256 devices in a mesh: tm: 8 (over y, core), tile: 32 (over x, z).
Axes of the slice: x: 4, y: 4, z: 8, core: 2. Of those that a mesh axis runs over, the one named last changes fastest.
Arguments:
- frames: bfloat16 [8, 4, 4096, 1024], P('tm', None, 'tile'), may hold values from -6 to 6
- peaks: int32 [8, 4, 2048], P('tm', None, 'tile'), may hold values from -10 to 10
- calib: float32 [12, 2048], P(None, 'tile'), may hold values from -1.25 to 1.25
- counts: int32 [32], P('tile'), may hold values from 16 to 64, as said below
- owner: int32 [2048, 1], P('tile'), may hold values from 0 to 31; in each aligned block of 64 rows (0 to 63, 64 to 127, ...) at most 4 rows name the same one
- cell: int32 [2048], P('tile'), may hold values from 0 to 2047
- spread: float32 [8, 2048], P(None, 'tile'), may hold values from 0.5 to 2
- start: int32 [1], replicated, may hold values from 0 to 4087
Outputs:
- spectrum: float32 [16, 6, 65536], P('tm', None, 'tile')
The draws below stay inside these ranges and needn't reach their ends.
Inputs may be any that keep to these rules, and one draw needn't show every extreme that they name: `counts`: the valid windows of a tile are its last ones in row-major order; some tile has all 64 valid. Among the 64 windows of one tile at most 4 name the same owner.
All inputs are finite; a program needn't handle non-finite values.
Results may differ from the reference program's by a relative error of at most 0.0003.
Values may be sent and summed in bfloat16 or wider, within the bound.
A program may use at most 64 MiB of HBM per device.

```python
import math
import jax
import jax.numpy as jnp
import numpy as np
from jax import lax

WIN = 64
IMG_W = 1024
FREQS = 16
NFFT = 4096
RADII = 128
AZ = 512
SPREAD = 8
SNAPS = 8
IMG_H = 4096
WT = 64
NWIN = 2048
CAP = 4
N_TILE = 32


def true_shifts(key):
    reach = WIN // 8
    shape = (SNAPS, 2, 2, IMG_H // (WIN // 2), IMG_W // WIN)
    return jax.random.randint(jax.random.fold_in(key, 101), shape, -reach, reach + 1)


def draw_frames(key, part):
    shifts = true_shifts(key)
    key = jax.random.fold_in(key, 1)
    base_key, noise_key = jax.random.split(key)
    shape = (SNAPS, 2, IMG_H, IMG_W)
    base = jax.random.truncated_normal(base_key, -4.0, 4.0, shape, jnp.float32)
    noise = jax.random.truncated_normal(noise_key, -4.0, 4.0, shape, jnp.float32)
    band = jnp.arange(IMG_H, dtype=jnp.int32) // (WIN // 2)
    column = jnp.arange(IMG_W, dtype=jnp.int32) // WIN

    def moved(pair):
        image, shift = pair
        shift_rows = shift[0][band][:, column]
        shift_cols = shift[1][band][:, column]
        rows = jnp.mod(jnp.arange(IMG_H, dtype=jnp.int32)[:, None] - shift_rows, IMG_H)
        cols = jnp.mod(jnp.arange(IMG_W, dtype=jnp.int32)[None, :] - shift_cols, IMG_W)
        return image[rows, cols]
    flat = lax.map(moved, (base.reshape(SNAPS * 2, IMG_H, IMG_W), shifts.reshape(SNAPS * 2, 2, IMG_H // (WIN // 2), IMG_W // WIN)))
    second = 0.8 * flat.reshape(shape) + 0.6 * noise
    frames = jnp.stack([base[:, 0], second[:, 0], base[:, 1], second[:, 1]], axis=1)
    return frames.astype(jnp.bfloat16)


def draw_peaks(key, part):
    shifts = true_shifts(key)
    key = jax.random.fold_in(key, 2)
    jitter = jax.random.randint(key, (SNAPS, 4, NWIN), -2, 3)
    return shifts.reshape(SNAPS, 4, NWIN) + jitter


def draw_counts(key, part):
    key = jax.random.fold_in(key, 3)
    values = jax.random.randint(key, (N_TILE,), WT // 4, WT + 1)
    chosen = jax.random.randint(jax.random.fold_in(key, 4), (), 0, N_TILE)
    return values.at[chosen].set(WT)


def plant(entries, key, low, top_value):
    longest = entries.shape.index(max(entries.shape))
    spots = []
    for shift in (0, 1):
        where = [jax.random.randint(jax.random.fold_in(key, axis), (), 0, length) for axis, length in enumerate(entries.shape)]
        where[longest] = (where[longest] + shift) % entries.shape[longest]
        spots.append(tuple(where))
    return entries.at[spots[0]].set(low).at[spots[1]].set(top_value)


def steps_of(own_key, shape, cuts, smallest, top_value):
    factor_of = 1.0
    for axis_at, blocks in cuts:
        draws = jax.random.uniform(jax.random.fold_in(jax.random.fold_in(own_key, 6), axis_at), (blocks,), jnp.float32, smallest / len(cuts), top_value / len(cuts))
        factor_of = factor_of * jnp.repeat(jnp.exp(draws), shape[axis_at] // blocks).reshape((-1,) + (1,) * (len(shape) - 1 - axis_at))
    return factor_of


def shared_out(key, own, number, rows, number_of, top, most, skew):
    ranking = jax.random.permutation(key, number_of)
    heavy_load, common = load_shares(number_of, rows * top, most, skew, True), load_shares(number_of, rows * top, most, skew, False)
    places = jnp.arange(number_of)

    def named(lengths, rotation):
        used = int((lengths > 0).sum())
        fixed = max(1, used // 4)
        moved = fixed + (places - fixed + rotation * (used - fixed)) % max(1, number_of - fixed)
        return jnp.zeros((number_of,), jnp.int32).at[ranking[jnp.where(places < fixed, places, moved)]].set(jnp.asarray(lengths, jnp.int32))

    lengths = jnp.where(number % 4 == 0, named(heavy_load, number // 4), named(common, number - number // 4 - 1))
    mixed = jax.random.permutation(jax.random.fold_in(own, 3), number_of)
    source_of, receiver = mixed[0:number_of // 2 * 2:2], mixed[1:number_of // 2 * 2:2]
    slack = jnp.minimum(lengths[source_of] - 1, most - lengths[receiver]) // 2
    slack = jnp.where((source_of == ranking[0]) | (receiver == ranking[0]) | (lengths[receiver] == 0), 0, jnp.maximum(slack, 0))
    moved = jax.random.randint(jax.random.fold_in(own, 4), (number_of // 2,), 0, 1 << 20) % (slack + 1)
    lengths = lengths.at[source_of].add(-moved).at[receiver].add(moved)
    labels = jnp.searchsorted(jnp.cumsum(lengths), jnp.arange(rows * top), side="right").astype(jnp.int32)
    grid = labels.reshape(top, rows).T
    grid = grid[jax.random.permutation(jax.random.fold_in(own, 1), rows)]
    rotation = jax.random.randint(jax.random.fold_in(own, 2), (rows, 1), 0, top)
    return jnp.take_along_axis(grid, (jnp.arange(top)[None, :] + rotation) % top, axis=1)


def load_shares(number_of, total, most, lean, full):
    portions = [(1 << 20) // math.isqrt(standing ** lean) + 1 for standing in range(1, number_of + 1)]
    largest = most if full else min(most, max(-(-total // number_of), total * portions[0] // sum(portions)))
    least = 1 if total - largest >= number_of - 1 else 0
    given, surplus = [largest] + [least] * (number_of - 1), total - largest - least * (number_of - 1)
    while surplus > 0:
        free = [i for i in range(1, number_of) if given[i] < largest] or [i for i in range(1, number_of) if given[i] < most]
        mass, left = sum([portions[i] for i in free]), surplus
        for i in free:
            extra = min(most - given[i], max(1, left * portions[i] // mass), surplus)
            given[i] = given[i] + extra
            surplus = surplus - extra
    return np.array(given)


def scatter_about(rng, extent, scale, most, shards=(), kind=jnp.bfloat16):
    result = scale * jax.random.normal(rng, extent, jnp.float32)
    if shards:
        result = result * steps_of(rng, extent, shards, -0.22, 0.18)
    return jnp.clip(result, -most, most).astype(kind)


def setup_inputs(seed: int = 0) -> dict:
    streams_of = jax.random.split(jax.random.key(seed), 9)
    frames = draw_frames(jax.random.fold_in(streams_of[8], 71), 0)
    peaks = draw_peaks(jax.random.fold_in(streams_of[8], 71), 0)
    calib = scatter_about(streams_of[2], (12, NWIN), 0.08, 1.25, ((1, 32),), jnp.float32)
    counts = draw_counts(jax.random.fold_in(streams_of[8], 71), 0)
    owner_keys = jax.random.split(jax.random.fold_in(streams_of[4], 1), NWIN // WT)
    owner_turns = jax.random.permutation(jax.random.fold_in(streams_of[4], 3), NWIN // WT)
    owner = jax.vmap(lambda own, number: shared_out(jax.random.fold_in(streams_of[4], 2), own, number, WT, N_TILE, 1, CAP, 2))(owner_keys, owner_turns).reshape((NWIN, 1))
    cell = plant(jax.random.randint(streams_of[5], (NWIN,), 0, RADII * AZ // N_TILE), jax.random.fold_in(streams_of[5], 1), 0, (RADII * AZ // N_TILE) - 1).astype(jnp.int32)
    spread = jnp.clip(jnp.exp(math.log(2.0) - 1.3862944 * jax.random.uniform(streams_of[6], (SPREAD, NWIN), jnp.float32) ** steps_of(streams_of[6], (SPREAD, NWIN), ((1, 32),), -0.2, 0.2)), 0.5, 2.0)
    start = jax.random.randint(streams_of[7], (1,), 0, NFFT - SNAPS).astype(jnp.int32)
    return dict(frames=frames, peaks=peaks, calib=calib, counts=counts, owner=owner, cell=cell, spread=spread, start=start)


sharpness = 20.0

def window_tiles(frame):
    count, height, width = frame.shape
    step = WIN // 2
    padded = jnp.pad(frame, ((0, 0), (0, step), (0, 0)))
    bands = padded.reshape(count, height // step + 1, step, width)
    rows = jnp.concatenate([bands[:, :-1], bands[:, 1:]], axis=2)
    tiles = rows.reshape(count, height // step, WIN, width // WIN, WIN)
    tiles = tiles.transpose(0, 1, 3, 2, 4)
    return tiles.reshape(count, height // step * (width // WIN), WIN, WIN)

def normalize(windows):
    centre = windows - lax.optimization_barrier(jnp.mean(windows, axis=(-2, -1), keepdims=True))
    spread_sq = lax.optimization_barrier(jnp.mean(centre * centre, axis=(-2, -1), keepdims=True))
    return centre / jnp.sqrt(spread_sq + 1e-05)

def subpixel(corr, peak_rows, peak_cols):
    size = corr.shape[-1]
    weights = jnp.exp(sharpness * corr)
    by_row = lax.optimization_barrier(jnp.sum(weights, axis=-1))
    by_col = lax.optimization_barrier(jnp.sum(weights, axis=-2))
    total = lax.optimization_barrier(jnp.sum(by_row, axis=-1))
    lags = jnp.arange(size, dtype=jnp.int32)
    off_rows = (jnp.mod(lags[None, :] - peak_rows[:, None] + size // 2, size) - size // 2).astype(jnp.float32)
    off_cols = (jnp.mod(lags[None, :] - peak_cols[:, None] + size // 2, size) - size // 2).astype(jnp.float32)
    disp_rows = peak_rows.astype(jnp.float32) + lax.optimization_barrier(jnp.sum(off_rows * by_row, axis=-1)) / total
    disp_cols = peak_cols.astype(jnp.float32) + lax.optimization_barrier(jnp.sum(off_cols * by_col, axis=-1)) / total
    return (disp_rows, disp_cols)

def per_snapshot(pair):
    frame, peak = pair
    normed = normalize(window_tiles(frame.astype(jnp.float32)))
    first = normed[0::2].reshape(-1, WIN, WIN)
    second = normed[1::2].reshape(-1, WIN, WIN)
    cross = jnp.conj(jnp.fft.fft2(first)) * jnp.fft.fft2(second)
    corr = jnp.real(jnp.fft.ifft2(cross)) / (WIN * WIN)
    disp_rows, disp_cols = subpixel(corr, peak[0::2].reshape(-1), peak[1::2].reshape(-1))
    disp_rows = disp_rows.reshape(2, -1)
    disp_cols = disp_cols.reshape(2, -1)
    return jnp.stack([disp_rows[0], disp_cols[0], disp_rows[1], disp_cols[1]])

def reference(frames, peaks, calib, counts, owner, cell, spread, start):
    disp = lax.map(per_snapshot, (frames, peaks))
    nwin = disp.shape[2]
    calib_three = calib.reshape(3, 4, nwin)
    vec = lax.optimization_barrier(jnp.sum(calib_three[None] * disp[:, None], axis=2))
    index = jnp.arange(nwin, dtype=jnp.int32)
    mask = (index % WT >= WT - counts[index // WT]).astype(jnp.float32)
    live = spread * mask[None]
    values = vec * mask[None, None]
    shift = jnp.arange(SPREAD, dtype=jnp.int32)[:, None]
    owner_cells = RADII * AZ // N_TILE
    targets = owner[:, 0][None] * owner_cells + cell[None] // AZ * AZ + jnp.mod(cell[None] % AZ + shift, AZ)
    targets = targets.reshape(-1)
    snaps = values.shape[0]
    terms = (live[None, None] * values[:, :, None, :]).reshape(snaps * 3, -1)
    num = jnp.zeros((snaps * 3, RADII * AZ), jnp.float32).at[:, targets].add(terms)
    den = jnp.zeros((RADII * AZ,), jnp.float32).at[targets].add(live.reshape(-1))
    field = (num / jnp.maximum(den, 1.0)[None]).reshape(snaps, 3, RADII * AZ)
    bins = jnp.arange(FREQS, dtype=jnp.int32) * (NFFT // FREQS)
    times = start[0] + jnp.arange(snaps, dtype=jnp.int32)
    phase = jnp.mod(bins[:, None] * times[None, :], NFFT).astype(jnp.float32) * (2.0 * math.pi / NFFT)
    real = jnp.einsum('fs,sic->fic', jnp.cos(phase), field, precision=lax.Precision.HIGHEST)
    imag = -jnp.einsum('fs,sic->fic', jnp.sin(phase), field, precision=lax.Precision.HIGHEST)
    return jnp.concatenate([real, imag], axis=1)
```

```python
import functools
import math

import jax
import jax.numpy as jnp
import ml_dtypes
import numpy as np
from jax import lax
from jax.experimental import pallas as pl
from jax.experimental.pallas import tpu as pltpu
from jax.sharding import PartitionSpec as P

WIN = 64
HALF = 32
FREQS = 16
NFFT = 4096
AZ = 512
SPREAD = 8
CAP = 4
GROUP = 256
WINS = 64
SHARPNESS = 20.0
MESH = pl.DeviceIdType.MESH
BF = jnp.bfloat16
F32 = jnp.float32
N_TM = 8
N_TILE = 32


def _pair(table):
    hi = table.astype(ml_dtypes.bfloat16)
    lo = (table - hi.astype(np.float64)).astype(ml_dtypes.bfloat16)
    return hi, lo


def _real_dft():
    n = np.arange(WIN)
    k = np.arange(HALF)[:, None]
    cos = np.round(np.cos(2.0 * np.pi * ((k * n) % WIN) / WIN), 14)
    sin = np.round(np.sin(2.0 * np.pi * ((k * n) % WIN) / WIN), 14)
    sin[0] = 1.0 - 2.0 * (n % 2)
    return cos, sin


def _tables():
    cos, sin = _real_dft()
    weight = np.where(np.arange(HALF) == 0, 1.0, 2.0)[:, None]
    eye = np.eye(4)
    fx = np.concatenate([np.kron(eye, cos.T), np.kron(eye, sin.T)], axis=1)
    ix = np.concatenate([np.kron(eye, weight * cos), np.kron(eye, weight * sin)], axis=0)
    fy = np.zeros((2, 3, HALF, 128))
    for r in range(3):
        fy[0, r, :, r * HALF : r * HALF + WIN] = cos
        fy[1, r, :, r * HALF : r * HALF + WIN] = sin
    fy = fy.reshape(192, 128)
    fyb = np.concatenate([cos, sin], axis=0)
    iy = np.concatenate([weight * cos, weight * sin], axis=0).T
    fx_hi, fx_lo = _pair(fx)
    ix_hi, ix_lo = _pair(ix)
    fy_hi, fy_lo = _pair(fy)
    fyb_hi, fyb_lo = _pair(fyb)
    iy_hi, iy_lo = _pair(iy)
    cat = np.concatenate
    return (
        np.stack([fx_hi, fx_lo]),
        np.stack([ix_hi, ix_lo]),
        cat([fy_hi, fy_hi], axis=1),
        fy_lo,
        cat([fyb_hi, fyb_hi, fyb_lo], axis=1),
        cat([iy_hi, iy_hi, iy_lo], axis=1),
    )


def dot(lhs, rhs):
    return jnp.dot(lhs, rhs, preferred_element_type=F32)


def dot_t(lhs, rhs):
    return lax.dot_general(lhs, rhs, (((1,), (1,)), ((), ())), preferred_element_type=F32)


def split2(x):
    hi = x.astype(BF)
    return hi, (x - hi.astype(F32)).astype(BF)


def split3(x):
    hi = x.astype(BF)
    rest = x - hi.astype(F32)
    mid = rest.astype(BF)
    return hi, mid, (rest - mid.astype(F32)).astype(BF)


def iota(shape, dim):
    return lax.broadcasted_iota(jnp.int32, shape, dim)


def cross(first, second, y0, x0):
    a, b, c, d = first
    a2, b2, c2, d2 = second
    aa, bb, cc, dd = a * a2, b * b2, c * c2, d * d2
    ac, bd = a * c2 - c * a2, b * d2 - d * b2
    ab, cd = a * b2 - b * a2, c * d2 - d * c2
    ad, bc = a * d2 + d * a2, b * c2 + c * b2
    low, high = jnp.where(x0, aa, aa + cc), jnp.where(x0, bb, bb + dd)
    low_s, high_s = jnp.where(x0, cc, ac), jnp.where(x0, dd, bd)
    p_cc = jnp.where(y0, low, low + high)
    p_cs = jnp.where(y0, low_s, jnp.where(x0, cc + dd, ac + bd))
    p_sc = jnp.where(y0, high, jnp.where(x0, ab, ab + cd))
    p_ss = jnp.where(y0, high_s, jnp.where(x0, cd, ad - bc))
    return p_cc, p_cs, p_sc, p_ss


def parts(t, half):
    return t[:half, :128], t[half:, :128], t[:half, 128:], t[half:, 128:]


def inverse_x(spectra, ix):
    rows = []
    for p_cc, p_cs, p_sc, p_ss in spectra:
        rows.append(jnp.concatenate([p_cc, p_cs], axis=1))
        rows.append(jnp.concatenate([p_sc, p_ss], axis=1))
    hi, lo = split2(jnp.concatenate(rows, axis=0))
    return dot(hi, ix[0]) + dot(lo, ix[0]) + dot(hi, ix[1])


def energy_rows(four, weight, bands):
    a, b, c, d = four
    e = (a * a + b * b) + (c * c + d * d)
    return [
        jnp.sum(e[r * HALF : (r + 1) * HALF] * weight, axis=0, keepdims=True) for r in range(bands)
    ]


def inverse_norm(rows, spread_lanes):
    have = len(rows)
    padded = rows + [jnp.zeros((16 - have, 128), F32)] * (have < 16)
    hi, mid, lo = split3(jnp.concatenate(padded, axis=0))
    wide = dot(jnp.concatenate([hi, mid, lo], axis=0), spread_lanes)
    total = wide[0:16] + wide[16:32] + wide[32:48]
    return lax.rsqrt(total * (1.0 / 4096.0**2) + 1e-5)


def wrapped(lag, peak):
    off = lag - peak
    return jnp.where(off >= 32.0, off - 64.0, off)


def correlate_and_send(
    frames, fx, ix, fy2, fy_lo, fyb, iy, peaks, calib, counts, owner, cell, spread, start,
    got_ref,
    image, halo, edge_hi, edge_lo, peak_lanes, stats, vecs, outbox, inbox,
    load_sem, halo_send, halo_recv, vec_send, vec_recv, box_send, box_recv,
):
    tm, tile = lax.axis_index("tm"), lax.axis_index("tile")
    above, below = lax.rem(tile + N_TILE - 1, N_TILE), lax.rem(tile + 1, N_TILE)

    load = pltpu.make_async_copy(frames.at[0], image, load_sem)
    load.start()

    barrier = pltpu.get_barrier_semaphore()

    def greet_tm(i, _):
        pl.semaphore_signal(
            barrier, 1, device_id=(lax.rem(tm + i, N_TM), tile), device_id_type=MESH
        )
        return _

    def greet_tile(i, _):
        pl.semaphore_signal(
            barrier, 1, device_id=(tm, lax.rem(tile + i, N_TILE)), device_id_type=MESH
        )
        return _

    lax.fori_loop(1, N_TM, greet_tm, 0)
    lax.fori_loop(1, N_TILE, greet_tile, 0)

    stats[...] = jnp.zeros_like(stats)
    peak = peaks[0].astype(F32)
    band_of = iota((4, WINS), 1) // 16
    picks = jnp.concatenate(
        [
            jnp.where(iota((4, WINS), 0) == band_of, jnp.broadcast_to(peak[j : j + 1], (4, WINS)), 0.0)
            for j in range(4)
        ],
        axis=0,
    ).astype(BF)
    to_lanes = (iota((WINS, 1024), 0) % 16 == iota((WINS, 1024), 1) // WIN).astype(F32).astype(BF)
    peak_lanes[...] = dot(picks, to_lanes)

    pl.semaphore_wait(barrier, N_TM + N_TILE - 2)
    halo_copy = pltpu.make_async_remote_copy(
        src_ref=frames.at[0, :, pl.ds(0, HALF), :],
        dst_ref=halo,
        send_sem=halo_send,
        recv_sem=halo_recv,
        device_id=(tm, above),
        device_id_type=MESH,
    )
    halo_copy.start()
    load.wait()

    weight = jnp.where(iota((HALF, 128), 0) == 0, 1.0, 2.0) * jnp.where(
        iota((HALF, 128), 1) % HALF == 0, 1.0, 2.0
    )
    spread_lanes = (iota((128, GROUP), 0) // HALF == iota((128, GROUP), 1) // WIN).astype(F32)
    spread_lanes = spread_lanes.astype(BF)
    row_lag = iota((WIN, GROUP), 0).astype(F32)
    col_lag = (iota((1, GROUP), 1) % WIN).astype(F32)
    gain = SHARPNESS * math.log2(math.e) / 4096.0**2

    def slots(bands):
        shape = (bands * HALF, 128)
        y0, x0 = iota(shape, 0) % HALF == 0, iota(shape, 1) % HALF == 0
        return y0, x0, y0 & x0

    def correlate(t, bands, first_band, lanes, span):
        half = bands * HALF
        y0, x0, dc = slots(bands)
        four = []
        for one in t:
            a, b, c, d = parts(one, half)
            four.append((jnp.where(dc, 0.0, a), b, c, d))
        energies = [row for one in four for row in energy_rows(one, weight, bands)]
        scale = inverse_norm(energies, spread_lanes)
        spectra = [cross(four[2 * cam], four[2 * cam + 1], y0, x0) for cam in range(2)]
        z_hi, z_lo = split2(inverse_x(spectra, ix))
        for cam in range(2):
            for r in range(bands):
                at = [(cam * 2 + part) * half + r * HALF for part in range(2)]
                hi = [z_hi[i : i + HALF] for i in at]
                lo = [z_lo[i : i + HALF] for i in at]
                corr = dot(iy[...], jnp.concatenate(hi + lo + hi, axis=0))
                i, j = (2 * cam) * bands + r, (2 * cam + 1) * bands + r
                p = jnp.exp2(corr * (scale[i : i + 1] * scale[j : j + 1] * gain))
                band = first_band + r
                i, j = 8 * cam + band, 8 * cam + 4 + band
                rows_at = peak_lanes[i : i + 1, pl.ds(lanes, span)]
                cols_at = peak_lanes[j : j + 1, pl.ds(lanes, span)]
                total = jnp.sum(p, axis=0, keepdims=True)
                by_row = jnp.sum(p * wrapped(row_lag, rows_at), axis=0, keepdims=True)
                by_col = total * wrapped(col_lag, cols_at)
                for k, value in enumerate((total, by_row, by_col)):
                    i = band * 8 + k * 2 + cam
                    stats[i : i + 1, pl.ds(lanes, span)] = value

    def own_bands(g, carry):
        lanes = pl.multiple_of(g * GROUP, GROUP)
        pixels = image[:, :, pl.ds(lanes, GROUP)].reshape(4 * 128, GROUP)
        x_hi, x_lo = split2(dot(pixels, fx[0]) + dot(pixels, fx[1]))
        t = []
        for f in range(4):
            hi, lo = x_hi[f * 128 : (f + 1) * 128], x_lo[f * 128 : (f + 1) * 128]
            edge_hi[f, :, pl.ds(lanes, GROUP)] = hi[96:]
            edge_lo[f, :, pl.ds(lanes, GROUP)] = lo[96:]
            t.append(dot(fy2[...], jnp.concatenate([hi, lo], axis=0)) + dot(fy_lo[...], hi))
        correlate(t, 3, 0, lanes, GROUP)
        return carry

    lax.fori_loop(0, 4, own_bands, 0)

    halo_copy.wait()

    def last_band(g, carry):
        lanes = pl.multiple_of(g * GROUP, GROUP)
        pixels = halo[:, :, pl.ds(lanes, GROUP)].reshape(4 * HALF, GROUP)
        x = dot(pixels, fx[0]) + dot(pixels, fx[1])
        x_hi, x_lo = split2(jnp.where(tile == N_TILE - 1, 0.0, x))
        t = []
        for f in range(4):
            hi = [edge_hi[f, :, pl.ds(lanes, GROUP)], x_hi[f * HALF : (f + 1) * HALF]]
            lo = [edge_lo[f, :, pl.ds(lanes, GROUP)], x_lo[f * HALF : (f + 1) * HALF]]
            t.append(dot(fyb[...], jnp.concatenate(hi + lo + hi, axis=0)))
        correlate(t, 1, 3, lanes, GROUP)
        return carry

    lax.fori_loop(0, 4, last_band, 0)

    lane = iota((8, 128), 1)
    window = lane % WINS
    to_window = (iota((1024, 128), 0) // WIN == iota((1024, 128), 1) % 16).astype(F32).astype(BF)
    hi, mid, lo = split3(stats[...])
    y = dot(jnp.concatenate([hi, mid, lo], axis=0), to_window)
    y = y[0:32] + y[32:64] + y[64:96]
    y = sum(jnp.where(window // 16 == r, y[8 * r : 8 * r + 8], 0.0) for r in range(4))
    peak2 = jnp.concatenate([peak, peak], axis=1)
    inverse = 1.0 / y[0:2]
    disp = []
    for cam in range(2):
        for part in range(2):
            j, i = 2 * cam + part, 2 + 2 * part + cam
            disp.append(peak2[j : j + 1] + y[i : i + 1] * inverse[cam : cam + 1])
    live = (window >= WINS - counts[0]).astype(F32)
    calib2 = jnp.concatenate([calib[...], calib[...]], axis=1)
    vec = []
    for i in range(3):
        vec.append(sum(calib2[4 * i + j : 4 * i + j + 1] * disp[j] for j in range(4)))
    six = jnp.concatenate(vec + vec + [jnp.zeros((2, 128), F32)], axis=0) * live
    vecs[pl.ds(tm, 1)] = six[None]

    def vec_copy(i):
        peer = lax.rem(tm + i, N_TM)
        return pltpu.make_async_remote_copy(
            src_ref=vecs.at[tm],
            dst_ref=vecs.at[tm],
            send_sem=vec_send,
            recv_sem=vec_recv,
            device_id=(peer, tile),
            device_id_type=MESH,
        )

    for i in range(1, N_TM):
        vec_copy(i).start()

    owners = jnp.concatenate([owner[...], owner[...]], axis=0)
    named = (owners == iota((128, 128), 1)).astype(F32)
    hits = named.T[0:N_TILE]
    before = ((iota((128, 128), 0) < iota((128, 128), 1) % WINS) & (iota((128, 128), 0) < WINS))
    earlier = dot(hits.astype(BF), before.astype(F32).astype(BF))
    rank = jnp.sum(hits * earlier, axis=0, keepdims=True)
    half = (iota((1, 128), 1) // WINS).astype(F32)
    place = jnp.concatenate(
        [jnp.where(rank == half, hits, 0.0), jnp.where(rank == half + 2.0, hits, 0.0)], axis=1
    ).astype(BF)
    cells = cell[...].astype(F32)
    cells = jnp.broadcast_to(jnp.concatenate([cells, cells], axis=1), (8, 128))
    spread2 = jnp.concatenate([spread[...], spread[...]], axis=1) * live
    part = iota((8, 128), 0)
    turn = jnp.where(part >= 3, 4, 0)
    coefs = []
    for k in range(2):
        freq = tm * 2 + k
        for s in range(N_TM):
            n = (freq * (start[0] + s) + turn) & 15
            value = jnp.zeros((8, 128), F32)
            for step in range(16):
                value = jnp.where(n == step, math.cos(2.0 * math.pi * step / 16), value)
            coefs.append(value)

    pltpu.make_async_copy(vecs.at[pl.ds(0, 7)], vecs.at[pl.ds(0, 7)], vec_send).wait()
    pltpu.make_async_copy(vecs.at[pl.ds(0, 7)], vecs.at[pl.ds(0, 7)], vec_recv).wait()
    fourier = [
        sum(coefs[k * N_TM + s] * vecs[s] for s in range(N_TM)) for k in range(2)
    ]
    fourier[0] = jnp.where(part == 6, 1.0, fourier[0])
    payload = jnp.concatenate(fourier + [spread2, cells], axis=0)
    first = iota((32, 128), 1) < WINS
    blank = jnp.zeros((WINS, 128), F32)
    both = jnp.concatenate(
        [jnp.where(first, payload, 0.0), jnp.where(first, 0.0, payload)], axis=0
    )
    table = jnp.concatenate(
        [jnp.concatenate([both, blank], axis=0), jnp.concatenate([blank, both], axis=0)], axis=1
    )
    message = sum(dot_t(place, piece) for piece in split3(table))
    outbox[...] = message.reshape(N_TILE, 1, 128)

    mine = pltpu.make_async_copy(outbox.at[tile], inbox.at[tile], load_sem)
    mine.start()

    def box_copy(i):
        peer = lax.rem(tile + i, N_TILE)
        return pltpu.make_async_remote_copy(
            src_ref=outbox.at[peer],
            dst_ref=inbox.at[tile],
            send_sem=box_send,
            recv_sem=box_recv,
            device_id=(tm, peer),
            device_id_type=MESH,
        )

    def send_box(i, carry):
        box_copy(i).start()
        return carry

    lax.fori_loop(1, N_TILE, send_box, 0)
    mine.wait()
    others = pl.ds(0, N_TILE - 1)
    pltpu.make_async_copy(outbox.at[others], outbox.at[others], box_send).wait()
    pltpu.make_async_copy(inbox.at[others], inbox.at[others], box_recv).wait()
    got_ref[...] = inbox[...].reshape(N_TILE, 128)


def deposit(got_ref, out_ref):
    got = got_ref[...]
    slots = jnp.concatenate(
        [got] + [pltpu.roll(got, 128 - 32 * c, 1) for c in range(1, CAP)], axis=0
    )
    cells = slots[:, 24:25].astype(jnp.int32)
    dist = (iota((128, AZ), 1) - cells) & (AZ - 1)
    weights = jnp.zeros((128, AZ), F32)
    for k in range(SPREAD):
        weights = jnp.where(dist == k, slots[:, 16 + k : 17 + k], weights)
    w_hi, w_lo = split2(weights)
    across = slots.T
    values = across[0:16]
    band = across[24:25].astype(jnp.int32) // AZ
    lhs_hi, lhs_lo = split2(
        jnp.concatenate([jnp.where(band == r, values, 0.0) for r in range(4)], axis=0)
    )
    num = dot(lhs_hi, w_hi) + dot(lhs_lo, w_hi) + dot(lhs_hi, w_lo)
    for r in range(4):
        block = num[16 * r : 16 * r + 16]
        scale = 1.0 / jnp.maximum(block[6:7], 1.0)
        out_ref[0, :, r * AZ : (r + 1) * AZ] = block[0:6] * scale
        out_ref[1, :, r * AZ : (r + 1) * AZ] = block[8:14] * scale


def on_device(frames, peaks, calib, counts, owner, cell, spread, start):
    tables = [jnp.asarray(t) for t in _tables()]
    vmem, smem = pl.BlockSpec(memory_space=pltpu.VMEM), pl.BlockSpec(memory_space=pltpu.SMEM)
    hbm = pl.BlockSpec(memory_space=pl.ANY)
    width = frames.shape[3]
    got = pl.pallas_call(
        correlate_and_send,
        out_shape=jax.ShapeDtypeStruct((N_TILE, 128), F32),
        in_specs=[hbm] + [vmem] * 6 + [vmem, vmem, smem, vmem, vmem, vmem, smem],
        out_specs=vmem,
        scratch_shapes=[
            pltpu.VMEM((4, 128, width), BF),
            pltpu.VMEM((4, HALF, width), BF),
            pltpu.VMEM((4, HALF, width), BF),
            pltpu.VMEM((4, HALF, width), BF),
            pltpu.VMEM((16, width), F32),
            pltpu.VMEM((32, width), F32),
            pltpu.VMEM((N_TM, 8, 128), F32),
            pltpu.VMEM((N_TILE, 1, 128), F32),
            pltpu.VMEM((N_TILE, 1, 128), F32),
        ]
        + [pltpu.SemaphoreType.DMA] * 7,
        compiler_params=pltpu.CompilerParams(
            collective_id=0, has_side_effects=True, vmem_limit_bytes=40 * 1024 * 1024
        ),
    )(frames, *tables, peaks, calib, counts, owner, cell.reshape(1, -1), spread, start)
    return pl.pallas_call(
        deposit,
        out_shape=jax.ShapeDtypeStruct((2, 6, 4 * AZ), F32),
        in_specs=[vmem],
        out_specs=vmem,
    )(got)


def solution(mesh):
    return jax.shard_map(
        on_device,
        mesh=mesh,
        in_specs=(
            P("tm", None, "tile", None),
            P("tm", None, "tile"),
            P(None, "tile"),
            P("tile"),
            P("tile", None),
            P("tile"),
            P(None, "tile"),
            P(),
        ),
        out_specs=P("tm", None, "tile"),
        check_vma=False,
    )
```

```python
import functools
import math

import jax
import jax.numpy as jnp
import ml_dtypes
import numpy as np
from jax import lax
from jax.experimental import pallas as pl
from jax.experimental.pallas import tpu as pltpu
from jax.sharding import PartitionSpec as P

WIN = 64
HALF = 32
FREQS = 16
NFFT = 4096
AZ = 512
SPREAD = 8
CAP = 4
GROUP = 256
WINS = 64
SHARPNESS = 20.0
MESH = pl.DeviceIdType.MESH
BF = jnp.bfloat16
F32 = jnp.float32
N_TM = 8
N_TILE = 32


def _pair(table):
    hi = table.astype(ml_dtypes.bfloat16)
    lo = (table - hi.astype(np.float64)).astype(ml_dtypes.bfloat16)
    return hi, lo


def _real_dft():
    n = np.arange(WIN)
    k = np.arange(HALF)[:, None]
    cos = np.round(np.cos(2.0 * np.pi * ((k * n) % WIN) / WIN), 14)
    sin = np.round(np.sin(2.0 * np.pi * ((k * n) % WIN) / WIN), 14)
    sin[0] = 1.0 - 2.0 * (n % 2)
    return cos, sin


def _tables():
    cos, sin = _real_dft()
    weight = np.where(np.arange(HALF) == 0, 1.0, 2.0)[:, None]
    eye = np.eye(4)
    fx = np.concatenate([np.kron(eye, cos.T), np.kron(eye, sin.T)], axis=1)
    ix = np.concatenate([np.kron(eye, weight * cos), np.kron(eye, weight * sin)], axis=0)
    fy = np.zeros((2, 3, HALF, 128))
    for r in range(3):
        fy[0, r, :, r * HALF : r * HALF + WIN] = cos
        fy[1, r, :, r * HALF : r * HALF + WIN] = sin
    fy = fy.reshape(192, 128)
    fyb = np.concatenate([cos, sin], axis=0)
    iy = np.concatenate([weight * cos, weight * sin], axis=0).T
    fx_hi, fx_lo = _pair(fx)
    ix_hi, ix_lo = _pair(ix)
    fy_hi, fy_lo = _pair(fy)
    fyb_hi, fyb_lo = _pair(fyb)
    iy_hi, iy_lo = _pair(iy)
    cat = np.concatenate
    return (
        np.stack([fx_hi, fx_lo]),
        np.stack([ix_hi, ix_lo]),
        cat([fy_hi, fy_hi], axis=1),
        fy_lo,
        cat([fyb_hi, fyb_hi, fyb_lo], axis=1),
        cat([iy_hi, iy_hi, iy_lo], axis=1),
    )


def dot(lhs, rhs):
    return jnp.dot(lhs, rhs, preferred_element_type=F32)


def dot_t(lhs, rhs):
    return lax.dot_general(lhs, rhs, (((1,), (1,)), ((), ())), preferred_element_type=F32)


def split2(x):
    hi = x.astype(BF)
    return hi, (x - hi.astype(F32)).astype(BF)


def split3(x):
    hi = x.astype(BF)
    rest = x - hi.astype(F32)
    mid = rest.astype(BF)
    return hi, mid, (rest - mid.astype(F32)).astype(BF)


def iota(shape, dim):
    return lax.broadcasted_iota(jnp.int32, shape, dim)


def cross(first, second, y0, x0):
    a, b, c, d = first
    a2, b2, c2, d2 = second
    aa, bb, cc, dd = a * a2, b * b2, c * c2, d * d2
    ac, bd = a * c2 - c * a2, b * d2 - d * b2
    ab, cd = a * b2 - b * a2, c * d2 - d * c2
    ad, bc = a * d2 + d * a2, b * c2 + c * b2
    low, high = jnp.where(x0, aa, aa + cc), jnp.where(x0, bb, bb + dd)
    low_s, high_s = jnp.where(x0, cc, ac), jnp.where(x0, dd, bd)
    p_cc = jnp.where(y0, low, low + high)
    p_cs = jnp.where(y0, low_s, jnp.where(x0, cc + dd, ac + bd))
    p_sc = jnp.where(y0, high, jnp.where(x0, ab, ab + cd))
    p_ss = jnp.where(y0, high_s, jnp.where(x0, cd, ad - bc))
    return p_cc, p_cs, p_sc, p_ss


def parts(t, half):
    return t[:half, :128], t[half:, :128], t[:half, 128:], t[half:, 128:]


def inverse_x(spectra, ix):
    rows = []
    for p_cc, p_cs, p_sc, p_ss in spectra:
        rows.append(jnp.concatenate([p_cc, p_cs], axis=1))
        rows.append(jnp.concatenate([p_sc, p_ss], axis=1))
    hi, lo = split2(jnp.concatenate(rows, axis=0))
    return dot(hi, ix[0]) + dot(lo, ix[0]) + dot(hi, ix[1])


def energy_rows(four, weight, bands):
    a, b, c, d = four
    e = (a * a + b * b) + (c * c + d * d)
    return [
        jnp.sum(e[r * HALF : (r + 1) * HALF] * weight, axis=0, keepdims=True) for r in range(bands)
    ]


def inverse_norm(rows, spread_lanes):
    have = len(rows)
    padded = rows + [jnp.zeros((16 - have, 128), F32)] * (have < 16)
    hi, mid, lo = split3(jnp.concatenate(padded, axis=0))
    wide = dot(jnp.concatenate([hi, mid, lo], axis=0), spread_lanes)
    total = wide[0:16] + wide[16:32] + wide[32:48]
    return lax.rsqrt(total * (1.0 / 4096.0**2) + 1e-5)


def wrapped(lag, peak):
    off = lag - peak
    return jnp.where(off >= 32.0, off - 64.0, off)


def correlate_and_send(
    frames, *refs,
):
    hbm_inputs, got_ref, inputs = refs[:12], refs[12], refs[13:25]
    fx, ix, fy2, fy_lo, fyb, iy, peaks, calib, scalars, owner, cell, spread = inputs
    image, halo, edge_hi, edge_lo, peak_lanes, stats, vecs, outbox, inbox = refs[25:34]
    load_sem, halo_send, halo_recv, vec_send, vec_recv, box_send, box_recv, input_sems = refs[34:]
    tm, tile = lax.axis_index("tm"), lax.axis_index("tile")
    above, below = lax.rem(tile + N_TILE - 1, N_TILE), lax.rem(tile + 1, N_TILE)

    loads = [
        pltpu.make_async_copy(source, target, input_sems.at[i])
        for i, (source, target) in enumerate(zip(hbm_inputs, inputs))
    ]
    load = pltpu.make_async_copy(frames.at[0], image, load_sem)
    for one in loads[6:]:
        one.start()
    load.start()
    for one in loads[:6]:
        one.start()

    barrier = pltpu.get_barrier_semaphore()

    def greet_tm(i, _):
        pl.semaphore_signal(
            barrier, 1, device_id=(lax.rem(tm + i, N_TM), tile), device_id_type=MESH
        )
        return _

    def greet_tile(i, _):
        pl.semaphore_signal(
            barrier, 1, device_id=(tm, lax.rem(tile + i, N_TILE)), device_id_type=MESH
        )
        return _

    lax.fori_loop(1, N_TM, greet_tm, 0)
    lax.fori_loop(1, N_TILE, greet_tile, 0)

    for one in loads[6:]:
        one.wait()

    stats[...] = jnp.zeros_like(stats)
    peak = peaks[0].astype(F32)
    band_of = iota((4, WINS), 1) // 16
    picks = jnp.concatenate(
        [
            jnp.where(iota((4, WINS), 0) == band_of, jnp.broadcast_to(peak[j : j + 1], (4, WINS)), 0.0)
            for j in range(4)
        ],
        axis=0,
    ).astype(BF)
    to_lanes = (iota((WINS, 1024), 0) % 16 == iota((WINS, 1024), 1) // WIN).astype(F32).astype(BF)
    peak_lanes[...] = dot(picks, to_lanes)

    pl.semaphore_wait(barrier, N_TM + N_TILE - 2)
    def halo_copy(g):
        lanes = pl.ds(g * GROUP, GROUP)
        return pltpu.make_async_remote_copy(
            src_ref=frames.at[0, :, pl.ds(0, HALF), lanes],
            dst_ref=halo.at[:, :, lanes],
            send_sem=halo_send.at[g],
            recv_sem=halo_recv.at[g],
            device_id=(tm, above),
            device_id_type=MESH,
        )

    for g in range(4):
        halo_copy(g).start()
    for one in loads[:6]:
        one.wait()
    load.wait()

    weight = jnp.where(iota((HALF, 128), 0) == 0, 1.0, 2.0) * jnp.where(
        iota((HALF, 128), 1) % HALF == 0, 1.0, 2.0
    )
    spread_lanes = (iota((128, GROUP), 0) // HALF == iota((128, GROUP), 1) // WIN).astype(F32)
    spread_lanes = spread_lanes.astype(BF)
    row_lag = iota((WIN, GROUP), 0).astype(F32)
    col_lag = (iota((1, GROUP), 1) % WIN).astype(F32)
    gain = SHARPNESS * math.log2(math.e) / 4096.0**2

    def slots(bands):
        shape = (bands * HALF, 128)
        y0, x0 = iota(shape, 0) % HALF == 0, iota(shape, 1) % HALF == 0
        return y0, x0, y0 & x0

    def correlate(t, bands, first_band, lanes, span):
        half = bands * HALF
        y0, x0, dc = slots(bands)
        four = []
        for one in t:
            a, b, c, d = parts(one, half)
            four.append((jnp.where(dc, 0.0, a), b, c, d))
        energies = [row for one in four for row in energy_rows(one, weight, bands)]
        scale = inverse_norm(energies, spread_lanes)
        spectra = [cross(four[2 * cam], four[2 * cam + 1], y0, x0) for cam in range(2)]
        z_hi, z_lo = split2(inverse_x(spectra, ix))
        for cam in range(2):
            for r in range(bands):
                at = [(cam * 2 + part) * half + r * HALF for part in range(2)]
                hi = [z_hi[i : i + HALF] for i in at]
                lo = [z_lo[i : i + HALF] for i in at]
                corr = dot(iy[...], jnp.concatenate(hi + lo + hi, axis=0))
                i, j = (2 * cam) * bands + r, (2 * cam + 1) * bands + r
                p = jnp.exp2(corr * (scale[i : i + 1] * scale[j : j + 1] * gain))
                band = first_band + r
                i, j = 8 * cam + band, 8 * cam + 4 + band
                rows_at = peak_lanes[i : i + 1, pl.ds(lanes, span)]
                cols_at = peak_lanes[j : j + 1, pl.ds(lanes, span)]
                total = jnp.sum(p, axis=0, keepdims=True)
                by_row = jnp.sum(p * wrapped(row_lag, rows_at), axis=0, keepdims=True)
                by_col = total * wrapped(col_lag, cols_at)
                for k, value in enumerate((total, by_row, by_col)):
                    i = band * 8 + k * 2 + cam
                    stats[i : i + 1, pl.ds(lanes, span)] = value

    def own_bands(g, carry):
        lanes = pl.multiple_of(g * GROUP, GROUP)
        pixels = image[:, :, pl.ds(lanes, GROUP)].reshape(4 * 128, GROUP)
        x_hi, x_lo = split2(dot(pixels, fx[0]) + dot(pixels, fx[1]))
        t = []
        for f in range(4):
            hi, lo = x_hi[f * 128 : (f + 1) * 128], x_lo[f * 128 : (f + 1) * 128]
            edge_hi[f, :, pl.ds(lanes, GROUP)] = hi[96:]
            edge_lo[f, :, pl.ds(lanes, GROUP)] = lo[96:]
            t.append(dot(fy2[...], jnp.concatenate([hi, lo], axis=0)) + dot(fy_lo[...], hi))
        correlate(t, 3, 0, lanes, GROUP)
        return carry

    lax.fori_loop(0, 4, own_bands, 0, unroll=True)


    def last_band(g, carry):
        halo_copy(g).wait()
        lanes = g * GROUP
        pixels = halo[:, :, pl.ds(lanes, GROUP)].reshape(4 * HALF, GROUP)
        x = dot(pixels, fx[0]) + dot(pixels, fx[1])
        x_hi, x_lo = split2(jnp.where(tile == N_TILE - 1, 0.0, x))
        t = []
        for f in range(4):
            hi = [edge_hi[f, :, pl.ds(lanes, GROUP)], x_hi[f * HALF : (f + 1) * HALF]]
            lo = [edge_lo[f, :, pl.ds(lanes, GROUP)], x_lo[f * HALF : (f + 1) * HALF]]
            t.append(dot(fyb[...], jnp.concatenate(hi + lo + hi, axis=0)))
        correlate(t, 1, 3, lanes, GROUP)
        return carry

    for g in range(4):
        last_band(g, 0)

    lane = iota((8, 128), 1)
    window = lane % WINS
    to_window = (iota((1024, 128), 0) // WIN == iota((1024, 128), 1) % 16).astype(F32).astype(BF)
    hi, mid, lo = split3(stats[...])
    y = dot(jnp.concatenate([hi, mid, lo], axis=0), to_window)
    y = y[0:32] + y[32:64] + y[64:96]
    y = sum(jnp.where(window // 16 == r, y[8 * r : 8 * r + 8], 0.0) for r in range(4))
    peak2 = jnp.concatenate([peak, peak], axis=1)
    inverse = 1.0 / y[0:2]
    disp = []
    for cam in range(2):
        for part in range(2):
            j, i = 2 * cam + part, 2 + 2 * part + cam
            disp.append(peak2[j : j + 1] + y[i : i + 1] * inverse[cam : cam + 1])
    live = (window >= WINS - scalars[:, 0:1]).astype(F32)
    calib2 = jnp.concatenate([calib[...], calib[...]], axis=1)
    vec = []
    for i in range(3):
        vec.append(sum(calib2[4 * i + j : 4 * i + j + 1] * disp[j] for j in range(4)))
        vec.append(vec[-1])
    six = jnp.concatenate(vec + [jnp.zeros((2, 128), F32)], axis=0) * live
    vecs[pl.ds(tm, 1)] = six[None]

    def vec_copy(i):
        peer = lax.rem(tm + i, N_TM)
        return pltpu.make_async_remote_copy(
            src_ref=vecs.at[tm],
            dst_ref=vecs.at[tm],
            send_sem=vec_send,
            recv_sem=vec_recv,
            device_id=(peer, tile),
            device_id_type=MESH,
        )

    for i in range(1, N_TM):
        vec_copy(i).start()

    owners = jnp.concatenate([owner[...], owner[...]], axis=1)
    hits = (owners == iota((N_TILE, 128), 0)).astype(F32)
    before = ((iota((128, 128), 0) < iota((128, 128), 1) % WINS) & (iota((128, 128), 0) < WINS))
    earlier = dot(hits.astype(BF), before.astype(F32).astype(BF))
    rank = jnp.sum(hits * earlier, axis=0, keepdims=True)
    half = (iota((1, 128), 1) // WINS).astype(F32)
    place = jnp.concatenate(
        [jnp.where(rank == half, hits, 0.0), jnp.where(rank == half + 2.0, hits, 0.0)], axis=1
    ).astype(BF)
    cells = cell[...].astype(F32)
    cells = jnp.broadcast_to(jnp.concatenate([cells, cells], axis=1), (8, 128))
    spread2 = jnp.concatenate([spread[...], spread[...]], axis=1) * live
    part = iota((8, 128), 0)
    freq = tm * 2 + (part & 1)
    coefs = []
    for k in range(2):
        for s in range(N_TM):
            n = (freq * (scalars[:, 1:2] + s) + 4 * k) & 15
            value = jnp.zeros((8, 128), F32)
            for step in range(16):
                value = jnp.where(n == step, math.cos(2.0 * math.pi * step / 16), value)
            coefs.append(value)

    pltpu.make_async_copy(vecs.at[pl.ds(0, 7)], vecs.at[pl.ds(0, 7)], vec_send).wait()
    pltpu.make_async_copy(vecs.at[pl.ds(0, 7)], vecs.at[pl.ds(0, 7)], vec_recv).wait()
    fourier = [
        sum(coefs[k * N_TM + s] * vecs[s] for s in range(N_TM)) for k in range(2)
    ]
    fourier[0] = jnp.where(part == 6, 1.0, fourier[0])
    payload = jnp.concatenate(fourier + [spread2, cells], axis=0)
    first = iota((32, 128), 1) < WINS
    blank = jnp.zeros((WINS, 128), F32)
    both = jnp.concatenate(
        [jnp.where(first, payload, 0.0), jnp.where(first, 0.0, payload)], axis=0
    )
    table = jnp.concatenate(
        [jnp.concatenate([both, blank], axis=0), jnp.concatenate([blank, both], axis=0)], axis=1
    )
    message = sum(dot_t(place, piece) for piece in split3(table))
    outbox[...] = message.reshape(N_TILE, 1, 128)

    mine = pltpu.make_async_copy(outbox.at[tile], inbox.at[tile], load_sem)
    mine.start()

    def box_copy(i):
        peer = lax.rem(tile + i, N_TILE)
        return pltpu.make_async_remote_copy(
            src_ref=outbox.at[peer],
            dst_ref=inbox.at[tile],
            send_sem=box_send,
            recv_sem=box_recv,
            device_id=(tm, peer),
            device_id_type=MESH,
        )

    def send_box(i, carry):
        box_copy(i).start()
        return carry

    lax.fori_loop(1, N_TILE, send_box, 0)
    mine.wait()
    others = pl.ds(0, N_TILE - 1)
    pltpu.make_async_copy(outbox.at[others], outbox.at[others], box_send).wait()
    pltpu.make_async_copy(inbox.at[others], inbox.at[others], box_recv).wait()
    got_ref[...] = inbox[...].reshape(N_TILE, 128)


def deposit(got_ref, out_ref):
    got = got_ref[...]
    slots = jnp.concatenate(
        [got] + [pltpu.roll(got, 128 - 32 * c, 1) for c in range(1, CAP)], axis=0
    )
    cells = slots[:, 24:25].astype(jnp.int32)
    dist = (iota((128, AZ), 1) - cells) & (AZ - 1)
    weights = jnp.zeros((128, AZ), F32)
    for k in range(SPREAD):
        weights = jnp.where(dist == k, slots[:, 16 + k : 17 + k], weights)
    w_hi, w_lo = split2(weights)
    across = slots.T
    values = across[0:16]
    band = across[24:25].astype(jnp.int32) // AZ
    lhs_hi, lhs_lo = split2(
        jnp.concatenate([jnp.where(band == r, values, 0.0) for r in range(4)], axis=0)
    )
    num = dot(lhs_hi, w_hi) + dot(lhs_lo, w_hi) + dot(lhs_hi, w_lo)
    for r in range(4):
        block = num[16 * r : 16 * r + 16]
        scale = 1.0 / jnp.maximum(block[6:7], 1.0)
        for k in range(2):
            terms = (block[8 * k : 8 * k + 6] * scale).reshape(3, 2, AZ)
            out_ref[3 * k : 3 * k + 3, :, r * AZ : (r + 1) * AZ] = terms


def on_device(frames, peaks, calib, counts, owner, cell, spread, start):
    tables = [jnp.asarray(t) for t in _tables()]
    vmem, hbm = pl.BlockSpec(memory_space=pltpu.VMEM), pl.BlockSpec(memory_space=pltpu.HBM)
    width = frames.shape[3]
    inputs = (
        *tables, peaks, calib, jnp.concatenate([counts, start]).reshape(1, 2), owner.reshape(1, -1),
        cell.reshape(1, -1), spread,
    )
    got = pl.pallas_call(
        correlate_and_send,
        out_shape=jax.ShapeDtypeStruct((N_TILE, 128), F32),
        in_specs=[hbm] * 13,
        out_specs=vmem,
        scratch_shapes=[
            pltpu.VMEM(x.shape, x.dtype) for x in inputs
        ]
        + [
            pltpu.VMEM((4, 128, width), BF),
            pltpu.VMEM((4, HALF, width), BF),
            pltpu.VMEM((4, HALF, width), BF),
            pltpu.VMEM((4, HALF, width), BF),
            pltpu.VMEM((16, width), F32),
            pltpu.VMEM((32, width), F32),
            pltpu.VMEM((N_TM, 8, 128), F32),
            pltpu.VMEM((N_TILE, 1, 128), F32),
            pltpu.VMEM((N_TILE, 1, 128), F32),
        ]
        + [pltpu.SemaphoreType.DMA, pltpu.SemaphoreType.DMA((4,)), pltpu.SemaphoreType.DMA((4,))]
        + [pltpu.SemaphoreType.DMA] * 4
        + [pltpu.SemaphoreType.DMA((12,))],
        compiler_params=pltpu.CompilerParams(
            collective_id=0, has_side_effects=True, vmem_limit_bytes=63 * 1024 * 1024
        ),
    )(frames, *inputs)
    spectrum = pl.pallas_call(
        deposit,
        out_shape=jax.ShapeDtypeStruct((6, 2, 4 * AZ), F32),
        in_specs=[vmem],
        out_specs=vmem,
        compiler_params=pltpu.CompilerParams(vmem_limit_bytes=63 * 1024 * 1024),
    )(got)
    return spectrum.transpose(1, 0, 2)


def solution(mesh):
    return jax.shard_map(
        on_device,
        mesh=mesh,
        in_specs=(
            P("tm", None, "tile", None),
            P("tm", None, "tile"),
            P(None, "tile"),
            P("tile"),
            P("tile", None),
            P("tile"),
            P(None, "tile"),
            P(),
        ),
        out_specs=P("tm", None, "tile"),
        check_vma=False,
    )
```

```python
import itertools
import math

import jax
import jax.numpy as jnp
import ml_dtypes
import numpy as np
from jax import lax
from jax.experimental import pallas as pl
from jax.experimental.pallas import tpu as pltpu
from jax.sharding import PartitionSpec as P

WIN = 64
HALF = 32
FREQS = 16
NFFT = 4096
AZ = 512
SPREAD = 8
CAP = 4
GROUP = 256
WINS = 64
SHARPNESS = 20.0
MESH = pl.DeviceIdType.MESH
BF = jnp.bfloat16
F32 = jnp.float32
N_TM = 8
N_TILE = 32


def _pair(table):
    hi = table.astype(ml_dtypes.bfloat16)
    lo = (table - hi.astype(np.float64)).astype(ml_dtypes.bfloat16)
    return hi, lo


def _real_dft():
    n = np.arange(WIN)
    k = np.arange(HALF)[:, None]
    cos = np.round(np.cos(2.0 * np.pi * ((k * n) % WIN) / WIN), 14)
    sin = np.round(np.sin(2.0 * np.pi * ((k * n) % WIN) / WIN), 14)
    sin[0] = 1.0 - 2.0 * (n % 2)
    return cos, sin


def _tables():
    cos, sin = _real_dft()
    weight = np.where(np.arange(HALF) == 0, 1.0, 2.0)[:, None]
    eye = np.eye(4)
    fx = np.concatenate([np.kron(eye, cos.T), np.kron(eye, sin.T)], axis=1)
    ix = np.concatenate([np.kron(eye, weight * cos), np.kron(eye, weight * sin)], axis=0)
    fy = np.zeros((2, 3, HALF, 128))
    for r in range(3):
        fy[0, r, :, r * HALF : r * HALF + WIN] = cos
        fy[1, r, :, r * HALF : r * HALF + WIN] = sin
    fy = fy.reshape(192, 128)
    fyb = np.concatenate([cos, sin], axis=0)
    iy = np.concatenate([weight * cos, weight * sin], axis=0).T
    fx_hi, fx_lo = _pair(fx)
    ix_hi, ix_lo = _pair(ix)
    fy_hi, fy_lo = _pair(fy)
    fyb_hi, fyb_lo = _pair(fyb)
    iy_hi, iy_lo = _pair(iy)
    cat = np.concatenate
    return (
        np.stack([fx_hi, fx_lo]),
        np.stack([ix_hi, ix_lo]),
        cat([fy_hi, fy_hi], axis=1),
        fy_lo,
        cat([fyb_hi, fyb_hi, fyb_lo], axis=1),
        cat([iy_hi, iy_hi, iy_lo], axis=1),
    )


def dot(lhs, rhs):
    return jnp.dot(lhs, rhs, preferred_element_type=F32)


def dot_t(lhs, rhs):
    return lax.dot_general(lhs, rhs, (((1,), (1,)), ((), ())), preferred_element_type=F32)


def split2(x):
    hi = x.astype(BF)
    return hi, (x - hi.astype(F32)).astype(BF)


def split3(x):
    hi = x.astype(BF)
    rest = x - hi.astype(F32)
    mid = rest.astype(BF)
    return hi, mid, (rest - mid.astype(F32)).astype(BF)


def iota(shape, dim):
    return lax.broadcasted_iota(jnp.int32, shape, dim)


def cross(first, second, y0, x0):
    a, b, c, d = first
    a2, b2, c2, d2 = second
    aa, bb, cc, dd = a * a2, b * b2, c * c2, d * d2
    ac, bd = a * c2 - c * a2, b * d2 - d * b2
    ab, cd = a * b2 - b * a2, c * d2 - d * c2
    ad, bc = a * d2 + d * a2, b * c2 + c * b2
    low, high = jnp.where(x0, aa, aa + cc), jnp.where(x0, bb, bb + dd)
    low_s, high_s = jnp.where(x0, cc, ac), jnp.where(x0, dd, bd)
    p_cc = jnp.where(y0, low, low + high)
    p_cs = jnp.where(y0, low_s, jnp.where(x0, cc + dd, ac + bd))
    p_sc = jnp.where(y0, high, jnp.where(x0, ab, ab + cd))
    p_ss = jnp.where(y0, high_s, jnp.where(x0, cd, ad - bc))
    return p_cc, p_cs, p_sc, p_ss


def parts(t, half):
    return t[:half, :128], t[half:, :128], t[:half, 128:], t[half:, 128:]


def inverse_x(spectra, ix):
    rows = []
    for p_cc, p_cs, p_sc, p_ss in spectra:
        rows.append(jnp.concatenate([p_cc, p_cs], axis=1))
        rows.append(jnp.concatenate([p_sc, p_ss], axis=1))
    hi, lo = split2(jnp.concatenate(rows, axis=0))
    return dot(hi, ix[0]) + dot(lo, ix[0]) + dot(hi, ix[1])


def energy_rows(four, weight, bands):
    a, b, c, d = four
    e = (a * a + b * b) + (c * c + d * d)
    return [
        jnp.sum(e[r * HALF : (r + 1) * HALF] * weight, axis=0, keepdims=True) for r in range(bands)
    ]


def inverse_norm(rows, spread_lanes):
    have = len(rows)
    padded = rows + [jnp.zeros((16 - have, 128), F32)] * (have < 16)
    hi, mid, lo = split3(jnp.concatenate(padded, axis=0))
    wide = dot(jnp.concatenate([hi, mid, lo], axis=0), spread_lanes)
    total = wide[0:16] + wide[16:32] + wide[32:48]
    return lax.rsqrt(total * (1.0 / 4096.0**2) + 1e-5)


def wrapped(lag, peak):
    off = lag - peak
    return jnp.where(off >= 32.0, off - 64.0, off)


def correlate_and_send(
    frames, *refs,
):
    hbm_inputs, got_ref, inputs = refs[:12], refs[12], refs[13:25]
    fx, ix, fy2, fy_lo, fyb, iy, peaks, calib, scalars, owner, cell, spread = inputs
    image, from_below, from_above, pack, pack_in, peak_lanes, stats, vecs, outbox, inbox = refs[25:35]
    load_sem, vec_send, vec_recv, box_send, box_recv, halo_send, halo_recv, input_sems, round_sem = (
        refs[35:]
    )
    tm, tile = lax.axis_index("tm"), lax.axis_index("tile")
    above, below = lax.rem(tile + N_TILE - 1, N_TILE), lax.rem(tile + 1, N_TILE)

    loads = [
        pltpu.make_async_copy(source, target, input_sems.at[i])
        for i, (source, target) in enumerate(zip(hbm_inputs, inputs))
    ]
    load = pltpu.make_async_copy(frames.at[0], image, load_sem)
    for one in loads[6:]:
        one.start()
    load.start()
    for one in loads[:6]:
        one.start()

    barrier = pltpu.get_barrier_semaphore()

    def greet(sem, d_tm, d_tile):
        peer = (lax.rem(tm + d_tm, N_TM), lax.rem(tile + d_tile, N_TILE))
        pl.semaphore_signal(sem, 1, device_id=peer, device_id_type=MESH)

    near = [d % N_TILE for i in range(1, 9) for d in (i, -i)]
    for d in near:
        greet(barrier, 0, d)
    for d in range(1, N_TM):
        greet(barrier, d, 0)

    pl.semaphore_wait(barrier, len(near) + N_TM - 1)
    for d in (8, N_TILE - 8):
        greet(round_sem, 0, d)
    def to_tile(peer, source, target, i):
        return pltpu.make_async_remote_copy(
            src_ref=source,
            dst_ref=target,
            send_sem=halo_send.at[i],
            recv_sem=halo_recv.at[i],
            device_id=(tm, peer),
            device_id_type=MESH,
        )

    halos = [
        to_tile(above, frames.at[0, pl.ds(0, 2), pl.ds(0, HALF), :], from_below, 0),
        to_tile(below, frames.at[0, pl.ds(2, 2), pl.ds(96, HALF), :], from_above, 1),
        to_tile(below, pack, pack_in, 2),
    ]
    halos[0].start()
    halos[1].start()
    for one in loads[6:]:
        one.wait()

    def twice(x):
        return jnp.concatenate([x, x], axis=1)

    window = iota((8, 128), 1) % WINS
    live = (window >= WINS - scalars[:, 0:1]).astype(F32)
    peak2, calib2 = twice(peaks[0].astype(F32)), twice(calib[...])
    owner2 = twice(owner[...].astype(F32))
    pack[0:16] = jnp.concatenate([calib2, peak2], axis=0)
    pack[16:24] = jnp.concatenate([owner2, live[0:7]], axis=0)
    halos[2].start()

    stats[...] = jnp.zeros_like(stats)
    band_of = iota((4, WINS), 1) // 16
    to_lanes = (iota((WINS, 1024), 0) % 16 == iota((WINS, 1024), 1) // WIN).astype(F32).astype(BF)

    def lanes_of_peaks(peak):
        picks = [
            jnp.where(
                iota((4, WINS), 0) == band_of, jnp.broadcast_to(peak[j : j + 1, :WINS], (4, WINS)), 0.0
            )
            for j in range(4)
        ]
        return dot(jnp.concatenate(picks, axis=0).astype(BF), to_lanes)

    peak_lanes[0:16] = lanes_of_peaks(peak2)

    for one in loads[:6]:
        one.wait()
    load.wait()

    weight = jnp.where(iota((HALF, 128), 0) == 0, 1.0, 2.0) * jnp.where(
        iota((HALF, 128), 1) % HALF == 0, 1.0, 2.0
    )
    spread_lanes = (iota((128, GROUP), 0) // HALF == iota((128, GROUP), 1) // WIN).astype(F32)
    spread_lanes = spread_lanes.astype(BF)
    row_lag = iota((WIN, GROUP), 0).astype(F32)
    col_lag = (iota((1, GROUP), 1) % WIN).astype(F32)
    gain = SHARPNESS * math.log2(math.e) / 4096.0**2

    def slots(bands):
        shape = (bands * HALF, 128)
        y0, x0 = iota(shape, 0) % HALF == 0, iota(shape, 1) % HALF == 0
        return y0, x0, y0 & x0

    def correlate(ts, bands, at_lanes, at_stats):
        half = bands * HALF
        y0, x0, dc = slots(bands)
        scales, spectra = [], []
        for t in ts:
            four = []
            for one in t:
                a, b, c, d = parts(one, half)
                four.append((jnp.where(dc, 0.0, a), b, c, d))
            energies = [row for one in four for row in energy_rows(one, weight, bands)]
            scales.append(inverse_norm(energies, spread_lanes))
            spectra += [cross(four[2 * cam], four[2 * cam + 1], y0, x0) for cam in range(2)]
        z_hi, z_lo = split2(inverse_x(spectra, ix))
        for g, cam, r in itertools.product(range(len(ts)), range(2), range(bands)):
            lanes, scale = slice(g * GROUP, (g + 1) * GROUP), scales[g]
            at = [((g * 2 + cam) * 2 + part) * half + r * HALF for part in range(2)]
            hi = [z_hi[i : i + HALF] for i in at]
            lo = [z_lo[i : i + HALF] for i in at]
            corr = dot(iy[...], jnp.concatenate(hi + lo + hi, axis=0))
            i, j = (2 * cam) * bands + r, (2 * cam + 1) * bands + r
            p = jnp.exp2(corr * (scale[i : i + 1] * scale[j : j + 1] * gain))
            i = at_lanes(cam, r)
            rows_at, cols_at = peak_lanes[i : i + 1, lanes], peak_lanes[i + 4 : i + 5, lanes]
            total = jnp.sum(p, axis=0, keepdims=True)
            by_row = jnp.sum(p * wrapped(row_lag, rows_at), axis=0, keepdims=True)
            by_col = total * wrapped(col_lag, cols_at)
            for k, value in enumerate((total, by_row, by_col)):
                i = at_stats(cam, r) * 8 + k * 2 + cam
                stats[i : i + 1, lanes] = value

    def x_transform(blocks):
        rows = [block[:, g * GROUP : (g + 1) * GROUP] for g in range(4) for block in blocks]
        pixels = jnp.concatenate(rows, axis=0)
        return dot(pixels, fx[0]) + dot(pixels, fx[1])

    x_hi, x_lo = split2(x_transform([image[f] for f in range(4)]))
    ts, edges = [], []
    for g in range(4):
        t = []
        for f in range(4):
            at = (g * 4 + f) * 128
            hi, lo = x_hi[at : at + 128], x_lo[at : at + 128]
            edges.append((hi[96:], lo[96:]) if f < 2 else (hi[:HALF], lo[:HALF]))
            t.append(dot(fy2[...], jnp.concatenate([hi, lo], axis=0)) + dot(fy_lo[...], hi))
        ts.append(t)
    correlate(ts, 3, lambda cam, r: 8 * cam + r, lambda cam, r: r)

    to_window = (iota((1024, 128), 0) // WIN == iota((1024, 128), 1) % 16).astype(F32).astype(BF)
    before = (iota((128, 128), 0) < iota((128, 128), 1) % WINS) & (iota((128, 128), 0) < WINS)
    before = before.astype(F32).astype(BF)
    half = (iota((1, 128), 1) // WINS).astype(F32)

    def places(owners):
        hits = (owners.astype(jnp.int32) == iota((N_TILE, 128), 0)).astype(F32)
        rank = jnp.sum(hits * dot(hits.astype(BF), before), axis=0, keepdims=True)
        both = [jnp.where(rank == half, hits, 0.0), jnp.where(rank == half + 2.0, hits, 0.0)]
        return jnp.concatenate(both, axis=1).astype(BF)

    place = places(owner2)
    cells = jnp.broadcast_to(twice(cell[...].astype(F32)), (8, 128))
    spread2 = twice(spread[...]) * live
    freq = tm * 2 + (iota((8, 128), 0) & 1)
    coefs = []
    for k in range(2):
        for s in range(N_TM):
            n = (freq * (scalars[:, 1:2] + s) + 4 * k) & 15
            value = jnp.zeros((8, 128), F32)
            for step in range(16):
                value = jnp.where(n == step, math.cos(2.0 * math.pi * step / 16), value)
            coefs.append(value)

    halos[2].wait()
    place_above = places(pack_in[16:17])
    peak_above, calib_above, live_above = pack_in[12:16], pack_in[0:12], pack_in[17:18]
    peak_lanes[16:32] = lanes_of_peaks(peak_above)

    halos[0].wait()
    halos[1].wait()
    x_hi, x_lo = split2(
        x_transform([from_below[0], from_below[1], from_above[0], from_above[1]])
    )
    last, first = tile == N_TILE - 1, tile == 0
    ts = []
    for g in range(4):
        t = []
        for f in range(4):
            at = (g * 4 + f) * HALF
            there = [x_hi[at : at + HALF], x_lo[at : at + HALF]]
            here = edges[g * 4 + f]
            if f < 2:
                there = [jnp.where(last, 0.0, x.astype(F32)).astype(BF) for x in there]
                hi, lo = [[a, b] for a, b in zip(here, there)]
            else:
                here = [jnp.where(first, 0.0, x.astype(F32)).astype(BF) for x in here]
                hi, lo = [[a, b] for a, b in zip(there, here)]
            t.append(dot(fyb[...], jnp.concatenate(hi + lo + hi, axis=0)))
        ts.append(t)
    correlate(ts, 1, lambda cam, r: 3 + 24 * cam, lambda cam, r: 3 + cam)

    hi, mid, lo = split3(stats[...])
    y = dot(jnp.concatenate([hi, mid, lo], axis=0), to_window)
    y = y[0:40] + y[40:80] + y[80:120]
    across = window[0:1] >= 48
    y_above = y[32:40]
    y = sum(jnp.where(window // 16 == r, y[8 * r : 8 * r + 8], 0.0) for r in range(4))

    def displacement(y, peak, cam):
        inverse = 1.0 / y[cam : cam + 1]
        return [
            peak[2 * cam + part : 2 * cam + part + 1]
            + y[2 + 2 * part + cam : 3 + 2 * part + cam] * inverse
            for part in range(2)
        ]

    def six_rows(calib, disp, live):
        vec = []
        for i in range(3):
            vec.append(sum(calib[4 * i + j : 4 * i + j + 1] * d for j, d in disp) * live)
            vec.append(vec[-1])
        return jnp.concatenate(vec + [jnp.zeros((2, 128), F32)], axis=0)

    disp = displacement(y, peak2, 0)
    disp += [jnp.where(across, 0.0, d) for d in displacement(y, peak2, 1)]
    own = six_rows(calib2, list(enumerate(disp)), live[0:1])
    disp = displacement(y_above, peak_above, 1)
    other = six_rows(calib_above, list(enumerate(disp, 2)), jnp.where(across, live_above, 0.0))
    vecs[pl.ds(tm, 1)] = jnp.concatenate([own, other], axis=0)[None]

    def vec_copy(i):
        peer = lax.rem(tm + i, N_TM)
        return pltpu.make_async_remote_copy(
            src_ref=vecs.at[tm],
            dst_ref=vecs.at[tm],
            send_sem=vec_send,
            recv_sem=vec_recv,
            device_id=(peer, tile),
            device_id_type=MESH,
        )

    for i in range(1, N_TM):
        vec_copy(i).start()

    pltpu.make_async_copy(vecs.at[pl.ds(0, 7)], vecs.at[pl.ds(0, 7)], vec_send).wait()
    pl.semaphore_wait(round_sem, 2)
    pltpu.make_async_copy(vecs.at[pl.ds(0, 7)], vecs.at[pl.ds(0, 7)], vec_recv).wait()
    def summed(k, rows):
        return sum(coefs[k * N_TM + s] * vecs[s, rows] for s in range(N_TM))

    first = iota((32, 128), 1) < WINS
    blank = jnp.zeros((WINS, 128), F32)

    def message(place, payload):
        both = jnp.concatenate(
            [jnp.where(first, payload, 0.0), jnp.where(first, 0.0, payload)], axis=0
        )
        table = jnp.concatenate(
            [jnp.concatenate([both, blank], axis=0), jnp.concatenate([blank, both], axis=0)], axis=1
        )
        return sum(dot_t(place, piece) for piece in split3(table))

    own, other = slice(0, 8), slice(8, 16)
    payload = jnp.concatenate([summed(0, own), summed(1, own), spread2, cells], axis=0)
    payload_above = jnp.concatenate(
        [summed(0, other), summed(1, other), jnp.zeros((16, 128), F32)], axis=0
    )
    outbox[:, 0:1] = message(place, payload).reshape(N_TILE, 1, 128)
    outbox[:, 1:2] = message(place_above, payload_above).reshape(N_TILE, 1, 128)

    mine = pltpu.make_async_copy(outbox.at[tile], inbox.at[tile], load_sem)
    mine.start()

    def box_copy(i):
        peer = lax.rem(tile + i, N_TILE)
        return pltpu.make_async_remote_copy(
            src_ref=outbox.at[peer],
            dst_ref=inbox.at[tile],
            send_sem=box_send,
            recv_sem=box_recv,
            device_id=(tm, peer),
            device_id_type=MESH,
        )

    def send_box(i, carry):
        box_copy(i).start()
        return carry

    lax.fori_loop(1, N_TILE, send_box, 0)
    mine.wait()
    others = pl.ds(0, N_TILE - 1)
    pltpu.make_async_copy(outbox.at[others], outbox.at[others], box_send).wait()
    pltpu.make_async_copy(inbox.at[others], inbox.at[others], box_recv).wait()
    first, second = inbox[:, 0], inbox[:, 1]
    got_ref[...] = first + jnp.concatenate([second[1:], second[:1]], axis=0)


def deposit(got_ref, out_ref):
    got = got_ref[...]
    slots = jnp.concatenate(
        [got] + [pltpu.roll(got, 128 - 32 * c, 1) for c in range(1, CAP)], axis=0
    )
    cells = slots[:, 24:25].astype(jnp.int32)
    dist = (iota((128, AZ), 1) - cells) & (AZ - 1)
    weights = jnp.zeros((128, AZ), F32)
    for k in range(SPREAD):
        weights = jnp.where(dist == k, slots[:, 16 + k : 17 + k], weights)
    w_hi, w_lo = split2(weights)
    across = slots.T
    values = jnp.where(iota((16, 128), 0) == 6, 1.0, across[0:16])
    band = across[24:25].astype(jnp.int32) // AZ
    lhs_hi, lhs_lo = split2(
        jnp.concatenate([jnp.where(band == r, values, 0.0) for r in range(4)], axis=0)
    )
    num = dot(lhs_hi, w_hi) + dot(lhs_lo, w_hi) + dot(lhs_hi, w_lo)
    for r in range(4):
        block = num[16 * r : 16 * r + 16]
        scale = 1.0 / jnp.maximum(block[6:7], 1.0)
        for k in range(2):
            terms = (block[8 * k : 8 * k + 6] * scale).reshape(3, 2, AZ)
            out_ref[3 * k : 3 * k + 3, :, r * AZ : (r + 1) * AZ] = terms


def on_device(frames, peaks, calib, counts, owner, cell, spread, start):
    tables = [jnp.asarray(t) for t in _tables()]
    vmem, hbm = pl.BlockSpec(memory_space=pltpu.VMEM), pl.BlockSpec(memory_space=pltpu.HBM)
    width = frames.shape[3]
    inputs = (
        *tables, peaks, calib, jnp.concatenate([counts, start]).reshape(1, 2), owner.reshape(1, -1),
        cell.reshape(1, -1), spread,
    )
    got = pl.pallas_call(
        correlate_and_send,
        out_shape=jax.ShapeDtypeStruct((N_TILE, 128), F32),
        in_specs=[hbm] * 13,
        out_specs=vmem,
        scratch_shapes=[
            pltpu.VMEM(x.shape, x.dtype) for x in inputs
        ]
        + [
            pltpu.VMEM((4, 128, width), BF),
            pltpu.VMEM((2, HALF, width), BF),
            pltpu.VMEM((2, HALF, width), BF),
            pltpu.VMEM((24, 128), F32),
            pltpu.VMEM((24, 128), F32),
            pltpu.VMEM((32, width), F32),
            pltpu.VMEM((40, width), F32),
            pltpu.VMEM((N_TM, 16, 128), F32),
            pltpu.VMEM((N_TILE, 2, 128), F32),
            pltpu.VMEM((N_TILE, 2, 128), F32),
        ]
        + [pltpu.SemaphoreType.DMA] * 5
        + [pltpu.SemaphoreType.DMA((3,))] * 2
        + [pltpu.SemaphoreType.DMA((12,)), pltpu.SemaphoreType.REGULAR],
        compiler_params=pltpu.CompilerParams(
            collective_id=0, has_side_effects=True, vmem_limit_bytes=63 * 1024 * 1024
        ),
    )(frames, *inputs)
    spectrum = pl.pallas_call(
        deposit,
        out_shape=jax.ShapeDtypeStruct((6, 2, 4 * AZ), F32),
        in_specs=[vmem],
        out_specs=vmem,
        compiler_params=pltpu.CompilerParams(vmem_limit_bytes=63 * 1024 * 1024),
    )(got)
    return spectrum.transpose(1, 0, 2)


def solution(mesh):
    return jax.shard_map(
        on_device,
        mesh=mesh,
        in_specs=(
            P("tm", None, "tile", None),
            P("tm", None, "tile"),
            P(None, "tile"),
            P("tile"),
            P("tile", None),
            P("tile"),
            P(None, "tile"),
            P(),
        ),
        out_specs=P("tm", None, "tile"),
        check_vma=False,
    )
```

```python
import itertools
import math

import jax
import jax.numpy as jnp
import ml_dtypes
import numpy as np
from jax import lax
from jax.experimental import pallas as pl
from jax.experimental.pallas import tpu as pltpu
from jax.sharding import PartitionSpec as P

WIN = 64
HALF = 32
FREQS = 16
NFFT = 4096
AZ = 512
SPREAD = 8
CAP = 4
GROUP = 256
WINS = 64
SHARPNESS = 20.0
MESH = pl.DeviceIdType.MESH
BF = jnp.bfloat16
F32 = jnp.float32
N_TM = 8
N_TILE = 32


def _pair(table):
    hi = table.astype(ml_dtypes.bfloat16)
    lo = (table - hi.astype(np.float64)).astype(ml_dtypes.bfloat16)
    return hi, lo


def _real_dft():
    n = np.arange(WIN)
    k = np.arange(HALF)[:, None]
    cos = np.round(np.cos(2.0 * np.pi * ((k * n) % WIN) / WIN), 14)
    sin = np.round(np.sin(2.0 * np.pi * ((k * n) % WIN) / WIN), 14)
    sin[0] = 1.0 - 2.0 * (n % 2)
    return cos, sin


def _tables():
    cos, sin = _real_dft()
    weight = np.where(np.arange(HALF) == 0, 1.0, 2.0)[:, None]
    eye = np.eye(4)
    fx = np.concatenate([np.kron(eye, cos.T), np.kron(eye, sin.T)], axis=1)
    ix = np.concatenate([np.kron(eye, weight * cos), np.kron(eye, weight * sin)], axis=0)
    fy = np.zeros((2, 3, HALF, 128))
    for r in range(3):
        fy[0, r, :, r * HALF : r * HALF + WIN] = cos
        fy[1, r, :, r * HALF : r * HALF + WIN] = sin
    fy = fy.reshape(192, 128)
    fyb = np.concatenate([cos, sin], axis=0)
    iy = np.concatenate([weight * cos, weight * sin], axis=0).T
    fx_hi, fx_lo = _pair(fx)
    ix_hi, ix_lo = _pair(ix)
    fy_hi, fy_lo = _pair(fy)
    fyb_hi, fyb_lo = _pair(fyb)
    iy_hi, iy_lo = _pair(iy)
    cat = np.concatenate
    return (
        np.stack([fx_hi, fx_lo]),
        np.stack([ix_hi, ix_lo]),
        cat([fy_hi, fy_hi], axis=1),
        fy_lo,
        cat([fyb_hi, fyb_hi, fyb_lo], axis=1),
        cat([iy_hi, iy_hi, iy_lo], axis=1),
    )


def dot(lhs, rhs):
    return jnp.dot(lhs, rhs, preferred_element_type=F32)


def dot_t(lhs, rhs):
    return lax.dot_general(lhs, rhs, (((1,), (1,)), ((), ())), preferred_element_type=F32)


def split2(x):
    hi = x.astype(BF)
    return hi, (x - hi.astype(F32)).astype(BF)


def split3(x):
    hi = x.astype(BF)
    rest = x - hi.astype(F32)
    mid = rest.astype(BF)
    return hi, mid, (rest - mid.astype(F32)).astype(BF)


def iota(shape, dim):
    return lax.broadcasted_iota(jnp.int32, shape, dim)


def cross(first, second, y0, x0):
    a, b, c, d = first
    a2, b2, c2, d2 = second
    aa, bb, cc, dd = a * a2, b * b2, c * c2, d * d2
    ac, bd = a * c2 - c * a2, b * d2 - d * b2
    ab, cd = a * b2 - b * a2, c * d2 - d * c2
    ad, bc = a * d2 + d * a2, b * c2 + c * b2
    low, high = jnp.where(x0, aa, aa + cc), jnp.where(x0, bb, bb + dd)
    low_s, high_s = jnp.where(x0, cc, ac), jnp.where(x0, dd, bd)
    p_cc = jnp.where(y0, low, low + high)
    p_cs = jnp.where(y0, low_s, jnp.where(x0, cc + dd, ac + bd))
    p_sc = jnp.where(y0, high, jnp.where(x0, ab, ab + cd))
    p_ss = jnp.where(y0, high_s, jnp.where(x0, cd, ad - bc))
    return p_cc, p_cs, p_sc, p_ss


def parts(t, half):
    return t[:half, :128], t[half:, :128], t[:half, 128:], t[half:, 128:]


def inverse_x(spectra, ix):
    rows = []
    for p_cc, p_cs, p_sc, p_ss in spectra:
        rows.append(jnp.concatenate([p_cc, p_cs], axis=1))
        rows.append(jnp.concatenate([p_sc, p_ss], axis=1))
    hi, lo = split2(jnp.concatenate(rows, axis=0))
    return dot(hi, ix[0]) + dot(lo, ix[0]) + dot(hi, ix[1])


def energy_rows(four, weight, bands):
    a, b, c, d = four
    e = (a * a + b * b) + (c * c + d * d)
    return [
        jnp.sum(e[r * HALF : (r + 1) * HALF] * weight, axis=0, keepdims=True) for r in range(bands)
    ]


def inverse_norm(rows, spread_lanes):
    have = len(rows)
    padded = rows + [jnp.zeros((16 - have, 128), F32)] * (have < 16)
    hi, mid, lo = split3(jnp.concatenate(padded, axis=0))
    wide = dot(jnp.concatenate([hi, mid, lo], axis=0), spread_lanes)
    total = wide[0:16] + wide[16:32] + wide[32:48]
    return lax.rsqrt(total * (1.0 / 4096.0**2) + 1e-5)


def wrapped(lag, peak):
    off = lag - peak
    return jnp.where(off >= 32.0, off - 64.0, off)


def correlate_and_send(
    counts, start, frames, *refs,
):
    hbm_inputs, got_ref, inputs = refs[:11], refs[11], refs[12:23]
    fx, ix, fy2, fy_lo, fyb, iy, peaks, calib, owner, cell, spread = inputs
    image, from_below, from_above, pack, pack_in, peak_lanes, stats, vecs, outbox, inbox = refs[23:33]
    load_sem, vec_send, vec_recv, box_send, box_recv, halo_send, halo_recv, input_sems, round_sem = (
        refs[33:]
    )
    tm, tile = lax.axis_index("tm"), lax.axis_index("tile")
    above, below = lax.rem(tile + N_TILE - 1, N_TILE), lax.rem(tile + 1, N_TILE)

    loads = [
        pltpu.make_async_copy(source, target, input_sems.at[i])
        for i, (source, target) in enumerate(zip(hbm_inputs, inputs))
    ]
    load = pltpu.make_async_copy(frames.at[0], image, load_sem)
    for one in loads[6:]:
        one.start()
    load.start()
    for one in loads[:6]:
        one.start()

    barrier = pltpu.get_barrier_semaphore()

    def greet(sem, d_tm, d_tile):
        peer = (lax.rem(tm + d_tm, N_TM), lax.rem(tile + d_tile, N_TILE))
        pl.semaphore_signal(sem, 1, device_id=peer, device_id_type=MESH)

    near = [d % N_TILE for i in range(1, 9) for d in (i, -i)]
    for d in near:
        greet(barrier, 0, d)
    for d in range(1, N_TM):
        greet(barrier, d, 0)

    pl.semaphore_wait(barrier, len(near) + N_TM - 1)
    for d in (8, N_TILE - 8):
        greet(round_sem, 0, d)
    def to_tile(peer, source, target, i):
        return pltpu.make_async_remote_copy(
            src_ref=source,
            dst_ref=target,
            send_sem=halo_send.at[i],
            recv_sem=halo_recv.at[i],
            device_id=(tm, peer),
            device_id_type=MESH,
        )

    halos = [
        to_tile(above, frames.at[0, pl.ds(0, 2), pl.ds(0, HALF), :], from_below, 0),
        to_tile(below, frames.at[0, pl.ds(2, 2), pl.ds(96, HALF), :], from_above, 1),
        to_tile(below, pack, pack_in, 2),
    ]
    halos[0].start()
    halos[1].start()
    for one in loads[6:]:
        one.wait()

    def twice(x):
        return jnp.concatenate([x, x], axis=1)

    window = iota((8, 128), 1) % WINS
    live = (window >= WINS - counts[0]).astype(F32)
    peak2, calib2 = twice(peaks[0].astype(F32)), twice(calib[...])
    owner2 = twice(owner[...].astype(F32))
    pack[0:16] = jnp.concatenate([calib2, peak2], axis=0)
    pack[16:24] = jnp.concatenate([owner2, live[0:7]], axis=0)
    halos[2].start()

    stats[...] = jnp.zeros_like(stats)
    band_of = iota((4, WINS), 1) // 16
    to_lanes = (iota((WINS, 1024), 0) % 16 == iota((WINS, 1024), 1) // WIN).astype(F32).astype(BF)

    def lanes_of_peaks(peak):
        picks = [
            jnp.where(
                iota((4, WINS), 0) == band_of, jnp.broadcast_to(peak[j : j + 1, :WINS], (4, WINS)), 0.0
            )
            for j in range(4)
        ]
        return dot(jnp.concatenate(picks, axis=0).astype(BF), to_lanes)

    peak_lanes[0:16] = lanes_of_peaks(peak2)

    for one in loads[:6]:
        one.wait()
    load.wait()

    weight = jnp.where(iota((HALF, 128), 0) == 0, 1.0, 2.0) * jnp.where(
        iota((HALF, 128), 1) % HALF == 0, 1.0, 2.0
    )
    spread_lanes = (iota((128, GROUP), 0) // HALF == iota((128, GROUP), 1) // WIN).astype(F32)
    spread_lanes = spread_lanes.astype(BF)
    row_lag = iota((WIN, GROUP), 0).astype(F32)
    col_lag = (iota((1, GROUP), 1) % WIN).astype(F32)
    gain = SHARPNESS * math.log2(math.e) / 4096.0**2

    def slots(bands):
        shape = (bands * HALF, 128)
        y0, x0 = iota(shape, 0) % HALF == 0, iota(shape, 1) % HALF == 0
        return y0, x0, y0 & x0

    def correlate(ts, bands, at_lanes, at_stats):
        half = bands * HALF
        y0, x0, dc = slots(bands)
        scales, spectra = [], []
        for t in ts:
            four = []
            for one in t:
                a, b, c, d = parts(one, half)
                four.append((jnp.where(dc, 0.0, a), b, c, d))
            energies = [row for one in four for row in energy_rows(one, weight, bands)]
            scales.append(inverse_norm(energies, spread_lanes))
            spectra += [cross(four[2 * cam], four[2 * cam + 1], y0, x0) for cam in range(2)]
        z_hi, z_lo = split2(inverse_x(spectra, ix))
        for g, cam, r in itertools.product(range(len(ts)), range(2), range(bands)):
            lanes, scale = slice(g * GROUP, (g + 1) * GROUP), scales[g]
            at = [((g * 2 + cam) * 2 + part) * half + r * HALF for part in range(2)]
            hi = [z_hi[i : i + HALF] for i in at]
            lo = [z_lo[i : i + HALF] for i in at]
            corr = dot(iy[...], jnp.concatenate(hi + lo + hi, axis=0))
            i, j = (2 * cam) * bands + r, (2 * cam + 1) * bands + r
            p = jnp.exp2(corr * (scale[i : i + 1] * scale[j : j + 1] * gain))
            i = at_lanes(cam, r)
            rows_at, cols_at = peak_lanes[i : i + 1, lanes], peak_lanes[i + 4 : i + 5, lanes]
            total = jnp.sum(p, axis=0, keepdims=True)
            by_row = jnp.sum(p * wrapped(row_lag, rows_at), axis=0, keepdims=True)
            by_col = total * wrapped(col_lag, cols_at)
            for k, value in enumerate((total, by_row, by_col)):
                i = at_stats(cam, r) * 8 + k * 2 + cam
                stats[i : i + 1, lanes] = value

    def x_transform(blocks):
        rows = [block[:, g * GROUP : (g + 1) * GROUP] for g in range(4) for block in blocks]
        pixels = jnp.concatenate(rows, axis=0)
        return dot(pixels, fx[0]) + dot(pixels, fx[1])

    x_hi, x_lo = split2(x_transform([image[f] for f in range(4)]))
    ts, edges = [], []
    for g in range(4):
        t = []
        for f in range(4):
            at = (g * 4 + f) * 128
            hi, lo = x_hi[at : at + 128], x_lo[at : at + 128]
            edges.append((hi[96:], lo[96:]) if f < 2 else (hi[:HALF], lo[:HALF]))
            t.append(dot(fy2[...], jnp.concatenate([hi, lo], axis=0)) + dot(fy_lo[...], hi))
        ts.append(t)
    correlate(ts, 3, lambda cam, r: 8 * cam + r, lambda cam, r: r)

    to_window = (iota((1024, 128), 0) // WIN == iota((1024, 128), 1) % 16).astype(F32).astype(BF)
    before = (iota((128, 128), 0) < iota((128, 128), 1) % WINS) & (iota((128, 128), 0) < WINS)
    before = before.astype(F32).astype(BF)
    half = (iota((1, 128), 1) // WINS).astype(F32)

    def places(owners):
        hits = (owners.astype(jnp.int32) == iota((N_TILE, 128), 0)).astype(F32)
        rank = jnp.sum(hits * dot(hits.astype(BF), before), axis=0, keepdims=True)
        both = [jnp.where(rank == half, hits, 0.0), jnp.where(rank == half + 2.0, hits, 0.0)]
        return jnp.concatenate(both, axis=1).astype(BF)

    place = places(owner2)
    cells = jnp.broadcast_to(twice(cell[...].astype(F32)), (8, 128))
    spread2 = twice(spread[...]) * live
    freq = tm * 2 + (iota((8, 128), 0) & 1)
    coefs = []
    for k in range(2):
        for s in range(N_TM):
            n = (freq * (start[0] + s) + 4 * k) & 15
            value = jnp.zeros((8, 128), F32)
            for step in range(16):
                value = jnp.where(n == step, math.cos(2.0 * math.pi * step / 16), value)
            coefs.append(value)

    halos[2].wait()
    place_above = places(pack_in[16:17])
    peak_above, calib_above, live_above = pack_in[12:16], pack_in[0:12], pack_in[17:18]
    peak_lanes[16:32] = lanes_of_peaks(peak_above)

    halos[0].wait()
    halos[1].wait()
    x_hi, x_lo = split2(
        x_transform([from_below[0], from_below[1], from_above[0], from_above[1]])
    )
    last, first = tile == N_TILE - 1, tile == 0
    ts = []
    for g in range(4):
        t = []
        for f in range(4):
            at = (g * 4 + f) * HALF
            there = [x_hi[at : at + HALF], x_lo[at : at + HALF]]
            here = edges[g * 4 + f]
            if f < 2:
                there = [jnp.where(last, 0.0, x.astype(F32)).astype(BF) for x in there]
                hi, lo = [[a, b] for a, b in zip(here, there)]
            else:
                here = [jnp.where(first, 0.0, x.astype(F32)).astype(BF) for x in here]
                hi, lo = [[a, b] for a, b in zip(there, here)]
            t.append(dot(fyb[...], jnp.concatenate(hi + lo + hi, axis=0)))
        ts.append(t)
    correlate(ts, 1, lambda cam, r: 3 + 24 * cam, lambda cam, r: 3 + cam)

    hi, mid, lo = split3(stats[...])
    y = dot(jnp.concatenate([hi, mid, lo], axis=0), to_window)
    y = y[0:40] + y[40:80] + y[80:120]
    across = window[0:1] >= 48
    y_above = y[32:40]
    y = sum(jnp.where(window // 16 == r, y[8 * r : 8 * r + 8], 0.0) for r in range(4))

    def displacement(y, peak, cam):
        inverse = 1.0 / y[cam : cam + 1]
        return [
            peak[2 * cam + part : 2 * cam + part + 1]
            + y[2 + 2 * part + cam : 3 + 2 * part + cam] * inverse
            for part in range(2)
        ]

    def six_rows(calib, disp, live):
        vec = []
        for i in range(3):
            vec.append(sum(calib[4 * i + j : 4 * i + j + 1] * d for j, d in disp) * live)
            vec.append(vec[-1])
        return jnp.concatenate(vec + [jnp.zeros((2, 128), F32)], axis=0)

    disp = displacement(y, peak2, 0)
    disp += [jnp.where(across, 0.0, d) for d in displacement(y, peak2, 1)]
    own = six_rows(calib2, list(enumerate(disp)), live[0:1])
    disp = displacement(y_above, peak_above, 1)
    other = six_rows(calib_above, list(enumerate(disp, 2)), jnp.where(across, live_above, 0.0))
    vecs[pl.ds(tm, 1)] = jnp.concatenate([own, other], axis=0)[None]

    def vec_copy(i):
        peer = lax.rem(tm + i, N_TM)
        return pltpu.make_async_remote_copy(
            src_ref=vecs.at[tm],
            dst_ref=vecs.at[tm],
            send_sem=vec_send,
            recv_sem=vec_recv,
            device_id=(peer, tile),
            device_id_type=MESH,
        )

    for i in range(1, N_TM):
        vec_copy(i).start()

    pltpu.make_async_copy(vecs.at[pl.ds(0, 7)], vecs.at[pl.ds(0, 7)], vec_send).wait()
    pl.semaphore_wait(round_sem, 2)
    pltpu.make_async_copy(vecs.at[pl.ds(0, 7)], vecs.at[pl.ds(0, 7)], vec_recv).wait()
    def summed(k, rows):
        return sum(coefs[k * N_TM + s] * vecs[s, rows] for s in range(N_TM))

    first = iota((32, 128), 1) < WINS
    blank = jnp.zeros((WINS, 128), F32)

    def message(place, payload):
        both = jnp.concatenate(
            [jnp.where(first, payload, 0.0), jnp.where(first, 0.0, payload)], axis=0
        )
        table = jnp.concatenate(
            [jnp.concatenate([both, blank], axis=0), jnp.concatenate([blank, both], axis=0)], axis=1
        )
        return sum(dot_t(place, piece) for piece in split2(table))

    own, other = slice(0, 8), slice(8, 16)
    payload = jnp.concatenate([summed(0, own), summed(1, own), spread2, cells], axis=0)
    payload_above = jnp.concatenate(
        [summed(0, other), summed(1, other), jnp.zeros((16, 128), F32)], axis=0
    )
    outbox[:, 0:1] = message(place, payload).reshape(N_TILE, 1, 128)
    outbox[:, 1:2] = message(place_above, payload_above).reshape(N_TILE, 1, 128)

    mine = pltpu.make_async_copy(outbox.at[tile], inbox.at[tile], load_sem)
    mine.start()

    def box_copy(i):
        peer = lax.rem(tile + i, N_TILE)
        return pltpu.make_async_remote_copy(
            src_ref=outbox.at[peer],
            dst_ref=inbox.at[tile],
            send_sem=box_send,
            recv_sem=box_recv,
            device_id=(tm, peer),
            device_id_type=MESH,
        )

    def send_box(i, carry):
        box_copy(i).start()
        return carry

    lax.fori_loop(1, N_TILE, send_box, 0)
    mine.wait()
    others = pl.ds(0, N_TILE - 1)
    pltpu.make_async_copy(outbox.at[others], outbox.at[others], box_send).wait()
    pltpu.make_async_copy(inbox.at[others], inbox.at[others], box_recv).wait()
    first, second = inbox[:, 0], inbox[:, 1]
    got_ref[...] = first + jnp.concatenate([second[1:], second[:1]], axis=0)


def deposit(got_ref, out_ref):
    got = got_ref[...]
    slots = jnp.concatenate(
        [got] + [pltpu.roll(got, 128 - 32 * c, 1) for c in range(1, CAP)], axis=0
    )
    cells = slots[:, 24:25].astype(jnp.int32)
    dist = (iota((128, AZ), 1) - cells) & (AZ - 1)
    weights = jnp.zeros((128, AZ), F32)
    for k in range(SPREAD):
        weights = jnp.where(dist == k, slots[:, 16 + k : 17 + k], weights)
    w_hi, w_lo = split2(weights)
    across = slots.T
    values = jnp.where(iota((16, 128), 0) == 6, 1.0, across[0:16])
    band = across[24:25].astype(jnp.int32) // AZ
    lhs_hi, lhs_lo = split2(
        jnp.concatenate([jnp.where(band == r, values, 0.0) for r in range(4)], axis=0)
    )
    num = dot(
        jnp.concatenate([lhs_hi, lhs_hi], axis=1), jnp.concatenate([w_hi, w_lo], axis=0)
    ) + dot(lhs_lo, w_hi)
    for r in range(4):
        block = num[16 * r : 16 * r + 16]
        scale = 1.0 / jnp.maximum(block[6:7], 1.0)
        for k in range(2):
            terms = (block[8 * k : 8 * k + 6] * scale).reshape(3, 2, AZ)
            out_ref[3 * k : 3 * k + 3, :, r * AZ : (r + 1) * AZ] = terms


def on_device(frames, peaks, calib, counts, owner, cell, spread, start):
    tables = [jnp.asarray(t) for t in _tables()]
    vmem, hbm = pl.BlockSpec(memory_space=pltpu.VMEM), pl.BlockSpec(memory_space=pltpu.HBM)
    smem = pl.BlockSpec(memory_space=pltpu.SMEM)
    width = frames.shape[3]
    inputs = (
        *tables, peaks, calib, owner.reshape(1, -1), cell.reshape(1, -1), spread
    )
    got = pl.pallas_call(
        correlate_and_send,
        out_shape=jax.ShapeDtypeStruct((N_TILE, 128), F32),
        in_specs=[smem, smem] + [hbm] * 12,
        out_specs=vmem,
        scratch_shapes=[
            pltpu.VMEM(x.shape, x.dtype) for x in inputs
        ]
        + [
            pltpu.VMEM((4, 128, width), BF),
            pltpu.VMEM((2, HALF, width), BF),
            pltpu.VMEM((2, HALF, width), BF),
            pltpu.VMEM((24, 128), F32),
            pltpu.VMEM((24, 128), F32),
            pltpu.VMEM((32, width), F32),
            pltpu.VMEM((40, width), F32),
            pltpu.VMEM((N_TM, 16, 128), F32),
            pltpu.VMEM((N_TILE, 2, 128), F32),
            pltpu.VMEM((N_TILE, 2, 128), F32),
        ]
        + [pltpu.SemaphoreType.DMA] * 5
        + [pltpu.SemaphoreType.DMA((3,))] * 2
        + [pltpu.SemaphoreType.DMA((11,)), pltpu.SemaphoreType.REGULAR],
        compiler_params=pltpu.CompilerParams(
            collective_id=0, has_side_effects=True, vmem_limit_bytes=63 * 1024 * 1024
        ),
    )(counts, start, frames, *inputs)
    spectrum = pl.pallas_call(
        deposit,
        out_shape=jax.ShapeDtypeStruct((6, 2, 4 * AZ), F32),
        in_specs=[vmem],
        out_specs=vmem,
        compiler_params=pltpu.CompilerParams(vmem_limit_bytes=63 * 1024 * 1024),
    )(got)
    return spectrum.transpose(1, 0, 2)


def solution(mesh):
    return jax.shard_map(
        on_device,
        mesh=mesh,
        in_specs=(
            P("tm", None, "tile", None),
            P("tm", None, "tile"),
            P(None, "tile"),
            P("tile"),
            P("tile", None),
            P("tile"),
            P(None, "tile"),
            P(),
        ),
        out_specs=P("tm", None, "tile"),
        check_vma=False,
    )
```

```python
import itertools
import math

import jax
import jax.numpy as jnp
import ml_dtypes
import numpy as np
from jax import lax
from jax.experimental import pallas as pl
from jax.experimental.pallas import tpu as pltpu
from jax.sharding import PartitionSpec as P

WIN = 64
HALF = 32
FREQS = 16
NFFT = 4096
AZ = 512
SPREAD = 8
CAP = 4
GROUP = 256
WINS = 64
SHARPNESS = 20.0
MESH = pl.DeviceIdType.MESH
BF = jnp.bfloat16
F32 = jnp.float32
N_TM = 8
N_TILE = 32


def _pair(table):
    hi = table.astype(ml_dtypes.bfloat16)
    lo = (table - hi.astype(np.float64)).astype(ml_dtypes.bfloat16)
    return hi, lo


def _real_dft():
    n = np.arange(WIN)
    k = np.arange(HALF)[:, None]
    cos = np.round(np.cos(2.0 * np.pi * ((k * n) % WIN) / WIN), 14)
    sin = np.round(np.sin(2.0 * np.pi * ((k * n) % WIN) / WIN), 14)
    sin[0] = 1.0 - 2.0 * (n % 2)
    return cos, sin


def _tables():
    cos, sin = _real_dft()
    weight = np.where(np.arange(HALF) == 0, 1.0, 2.0)[:, None]
    eye = np.eye(4)
    fx = np.concatenate([np.kron(eye, cos.T), np.kron(eye, sin.T)], axis=1)
    ix = np.concatenate([np.kron(eye, weight * cos), np.kron(eye, weight * sin)], axis=0)
    fy = np.zeros((2, 3, HALF, 128))
    for r in range(3):
        fy[0, r, :, r * HALF : r * HALF + WIN] = cos
        fy[1, r, :, r * HALF : r * HALF + WIN] = sin
    fy = fy.reshape(192, 128)
    fyb = np.concatenate([cos, sin], axis=0)
    iy = np.concatenate([weight * cos, weight * sin], axis=0).T
    fx_hi, fx_lo = _pair(fx)
    ix_hi, ix_lo = _pair(ix)
    fy_hi, fy_lo = _pair(fy)
    fyb_hi, fyb_lo = _pair(fyb)
    iy_hi, iy_lo = _pair(iy)
    cat = np.concatenate
    return (
        np.stack([fx_hi, fx_lo]),
        np.stack([ix_hi, ix_lo]),
        cat([fy_hi, fy_hi], axis=1),
        fy_lo,
        cat([fyb_hi, fyb_hi, fyb_lo], axis=1),
        cat([iy_hi, iy_hi, iy_lo], axis=1),
    )


def dot(lhs, rhs):
    return jnp.dot(lhs, rhs, preferred_element_type=F32)


def dot_t(lhs, rhs):
    return lax.dot_general(lhs, rhs, (((1,), (1,)), ((), ())), preferred_element_type=F32)


def split2(x):
    hi = x.astype(BF)
    return hi, (x - hi.astype(F32)).astype(BF)


def split3(x):
    hi = x.astype(BF)
    rest = x - hi.astype(F32)
    mid = rest.astype(BF)
    return hi, mid, (rest - mid.astype(F32)).astype(BF)


def iota(shape, dim):
    return lax.broadcasted_iota(jnp.int32, shape, dim)


def cross(first, second, y0, x0):
    a, b, c, d = first
    a2, b2, c2, d2 = second
    aa, bb, cc, dd = a * a2, b * b2, c * c2, d * d2
    ac, bd = a * c2 - c * a2, b * d2 - d * b2
    ab, cd = a * b2 - b * a2, c * d2 - d * c2
    ad, bc = a * d2 + d * a2, b * c2 + c * b2
    low, high = jnp.where(x0, aa, aa + cc), jnp.where(x0, bb, bb + dd)
    low_s, high_s = jnp.where(x0, cc, ac), jnp.where(x0, dd, bd)
    p_cc = jnp.where(y0, low, low + high)
    p_cs = jnp.where(y0, low_s, jnp.where(x0, cc + dd, ac + bd))
    p_sc = jnp.where(y0, high, jnp.where(x0, ab, ab + cd))
    p_ss = jnp.where(y0, high_s, jnp.where(x0, cd, ad - bc))
    return p_cc, p_cs, p_sc, p_ss


def parts(t, half):
    return t[:half, :128], t[half:, :128], t[:half, 128:], t[half:, 128:]


def inverse_x(spectra, ix):
    rows = []
    for p_cc, p_cs, p_sc, p_ss in spectra:
        rows.append(jnp.concatenate([p_cc, p_cs], axis=1))
        rows.append(jnp.concatenate([p_sc, p_ss], axis=1))
    hi, lo = split2(jnp.concatenate(rows, axis=0))
    return dot(hi, ix[0]) + dot(lo, ix[0]) + dot(hi, ix[1])


def energy_rows(four, weight, bands):
    a, b, c, d = four
    e = (a * a + b * b) + (c * c + d * d)
    return [
        jnp.sum(e[r * HALF : (r + 1) * HALF] * weight, axis=0, keepdims=True) for r in range(bands)
    ]


def inverse_norm(rows, spread_lanes):
    have = len(rows)
    padded = rows + [jnp.zeros((16 - have, 128), F32)] * (have < 16)
    hi, mid, lo = split3(jnp.concatenate(padded, axis=0))
    wide = dot(jnp.concatenate([hi, mid, lo], axis=0), spread_lanes)
    total = wide[0:16] + wide[16:32] + wide[32:48]
    return lax.rsqrt(total * (1.0 / 4096.0**2) + 1e-5)


def wrapped(lag, peak):
    off = lag - peak
    return jnp.where(off >= 32.0, off - 64.0, off)


def correlate_and_send(
    counts, start, frames, *refs,
):
    hbm_inputs, got_ref, inputs = refs[:11], refs[11], refs[12:23]
    fx, ix, fy2, fy_lo, fyb, iy, peaks, calib, owner, cell, spread = inputs
    image, from_below, from_above, pack, pack_in, peak_lanes, stats, vecs, outbox, inbox = refs[23:33]
    load_sem, vec_send, vec_recv, box_send, box_recv, halo_send, halo_recv, input_sems, round_sem = (
        refs[33:]
    )
    tm, tile = lax.axis_index("tm"), lax.axis_index("tile")
    above, below = lax.rem(tile + N_TILE - 1, N_TILE), lax.rem(tile + 1, N_TILE)

    loads = [
        pltpu.make_async_copy(source, target, input_sems.at[i])
        for i, (source, target) in enumerate(zip(hbm_inputs, inputs))
    ]
    load = pltpu.make_async_copy(frames.at[0], image, load_sem)
    for one in loads[6:]:
        one.start()
    load.start()
    for one in loads[:6]:
        one.start()

    barrier = pltpu.get_barrier_semaphore()

    def greet(sem, d_tm, d_tile):
        peer = (lax.rem(tm + d_tm, N_TM), lax.rem(tile + d_tile, N_TILE))
        pl.semaphore_signal(sem, 1, device_id=peer, device_id_type=MESH)

    near = [d % N_TILE for i in range(1, 9) for d in (i, -i)]
    for d in near:
        greet(barrier, 0, d)
    for d in range(1, N_TM):
        greet(barrier, d, 0)

    pl.semaphore_wait(barrier, len(near) + N_TM - 1)
    for d in (8, N_TILE - 8):
        greet(round_sem, 0, d)
    def to_tile(peer, source, target, i):
        return pltpu.make_async_remote_copy(
            src_ref=source,
            dst_ref=target,
            send_sem=halo_send.at[i],
            recv_sem=halo_recv.at[i],
            device_id=(tm, peer),
            device_id_type=MESH,
        )

    halos = [
        to_tile(above, frames.at[0, pl.ds(0, 2), pl.ds(0, HALF), :], from_below, 0),
        to_tile(below, frames.at[0, pl.ds(2, 2), pl.ds(96, HALF), :], from_above, 1),
        to_tile(below, pack, pack_in, 2),
    ]
    halos[0].start()
    halos[1].start()
    for one in loads[6:]:
        one.wait()

    def twice(x):
        return jnp.concatenate([x, x], axis=1)

    window = iota((8, 128), 1) % WINS
    live = (window >= WINS - counts[0]).astype(F32)
    peak2, calib2 = twice(peaks[0].astype(F32)), twice(calib[...])
    owner2 = twice(owner[...].astype(F32))
    pack[0:16] = jnp.concatenate([calib2, peak2], axis=0)
    pack[16:24] = jnp.concatenate([owner2, live[0:7]], axis=0)
    halos[2].start()

    stats[...] = jnp.zeros_like(stats)
    band_of = iota((4, WINS), 1) // 16
    to_lanes = (iota((WINS, 1024), 0) % 16 == iota((WINS, 1024), 1) // WIN).astype(F32).astype(BF)

    def lanes_of_peaks(peak):
        picks = [
            jnp.where(
                iota((4, WINS), 0) == band_of, jnp.broadcast_to(peak[j : j + 1, :WINS], (4, WINS)), 0.0
            )
            for j in range(4)
        ]
        return dot(jnp.concatenate(picks, axis=0).astype(BF), to_lanes)

    peak_lanes[0:16] = lanes_of_peaks(peak2)

    for one in loads[:6]:
        one.wait()
    load.wait()

    weight = jnp.where(iota((HALF, 128), 0) == 0, 1.0, 2.0) * jnp.where(
        iota((HALF, 128), 1) % HALF == 0, 1.0, 2.0
    )
    spread_lanes = (iota((128, GROUP), 0) // HALF == iota((128, GROUP), 1) // WIN).astype(F32)
    spread_lanes = spread_lanes.astype(BF)
    row_lag = iota((WIN, GROUP), 0).astype(F32)
    col_lag = (iota((1, GROUP), 1) % WIN).astype(F32)
    gain = SHARPNESS * math.log2(math.e) / 4096.0**2

    def slots(bands):
        shape = (bands * HALF, 128)
        y0, x0 = iota(shape, 0) % HALF == 0, iota(shape, 1) % HALF == 0
        return y0, x0, y0 & x0

    def correlate(ts, bands, at_lanes, at_stats):
        half = bands * HALF
        y0, x0, dc = slots(bands)
        scales, spectra = [], []
        for t in ts:
            four = []
            for one in t:
                a, b, c, d = parts(one, half)
                four.append((jnp.where(dc, 0.0, a), b, c, d))
            energies = [row for one in four for row in energy_rows(one, weight, bands)]
            scales.append(inverse_norm(energies, spread_lanes))
            spectra += [cross(four[2 * cam], four[2 * cam + 1], y0, x0) for cam in range(2)]
        z_hi, z_lo = split2(inverse_x(spectra, ix))
        for g, cam, r in itertools.product(range(len(ts)), range(2), range(bands)):
            lanes, scale = slice(g * GROUP, (g + 1) * GROUP), scales[g]
            at = [((g * 2 + cam) * 2 + part) * half + r * HALF for part in range(2)]
            hi = [z_hi[i : i + HALF] for i in at]
            lo = [z_lo[i : i + HALF] for i in at]
            corr = dot(iy[...], jnp.concatenate(hi + lo + hi, axis=0))
            i, j = (2 * cam) * bands + r, (2 * cam + 1) * bands + r
            p = jnp.exp2(corr * (scale[i : i + 1] * scale[j : j + 1] * gain))
            i = at_lanes(cam, r)
            rows_at, cols_at = peak_lanes[i : i + 1, lanes], peak_lanes[i + 4 : i + 5, lanes]
            total = jnp.sum(p, axis=0, keepdims=True)
            by_row = jnp.sum(p * wrapped(row_lag, rows_at), axis=0, keepdims=True)
            by_col = total * wrapped(col_lag, cols_at)
            for k, value in enumerate((total, by_row, by_col)):
                i = at_stats(cam, r) * 8 + k * 2 + cam
                stats[i : i + 1, lanes] = value

    def x_transform(blocks):
        rows = [block[:, g * GROUP : (g + 1) * GROUP] for g in range(4) for block in blocks]
        pixels = jnp.concatenate(rows, axis=0)
        return dot(pixels, fx[0]) + dot(pixels, fx[1])

    last, first = tile == N_TILE - 1, tile == 0
    mean_lane = (iota((1, GROUP), 1) < 128) & (iota((1, GROUP), 1) % HALF == 0)
    x = x_transform([image[f] for f in range(4)])
    ts, edges, levels = [], [], []
    for g in range(4):
        t = []
        for f in range(4):
            at = (g * 4 + f) * 128
            level = jnp.where(mean_lane, x[at : at + 1], 0.0)
            hi, lo = split2(x[at : at + 128] - level)
            levels.append(level)
            top = jnp.where(first, 0.0, x[at : at + HALF]) - level
            edges.append((hi[96:], lo[96:]) if f < 2 else split2(top))
            t.append(dot(fy2[...], jnp.concatenate([hi, lo], axis=0)) + dot(fy_lo[...], hi))
        ts.append(t)
    correlate(ts, 3, lambda cam, r: 8 * cam + r, lambda cam, r: r)

    to_window = (iota((1024, 128), 0) // WIN == iota((1024, 128), 1) % 16).astype(F32).astype(BF)
    before = (iota((128, 128), 0) < iota((128, 128), 1) % WINS) & (iota((128, 128), 0) < WINS)
    before = before.astype(F32).astype(BF)
    half = (iota((1, 128), 1) // WINS).astype(F32)

    def places(owners):
        hits = (owners.astype(jnp.int32) == iota((N_TILE, 128), 0)).astype(F32)
        rank = jnp.sum(hits * dot(hits.astype(BF), before), axis=0, keepdims=True)
        both = [jnp.where(rank == half, hits, 0.0), jnp.where(rank == half + 2.0, hits, 0.0)]
        return jnp.concatenate(both, axis=1).astype(BF)

    place = places(owner2)
    cells = jnp.broadcast_to(twice(cell[...].astype(F32)), (8, 128))
    spread2 = twice(spread[...]) * live
    freq = tm * 2 + (iota((8, 128), 0) & 1)
    coefs = []
    for k in range(2):
        for s in range(N_TM):
            n = (freq * (start[0] + s) + 4 * k) & 15
            value = jnp.zeros((8, 128), F32)
            for step in range(16):
                value = jnp.where(n == step, math.cos(2.0 * math.pi * step / 16), value)
            coefs.append(value)

    halos[2].wait()
    place_above = places(pack_in[16:17])
    peak_above, calib_above, live_above = pack_in[12:16], pack_in[0:12], pack_in[17:18]
    peak_lanes[16:32] = lanes_of_peaks(peak_above)

    halos[0].wait()
    halos[1].wait()
    x = x_transform([from_below[0], from_below[1], from_above[0], from_above[1]])
    keep = jnp.where(last, 0.0, 1.0)
    ts = []
    for g in range(4):
        t = []
        for f in range(4):
            i = g * 4 + f
            part = x[i * HALF : (i + 1) * HALF]
            there = split2((part * keep if f < 2 else part) - levels[i])
            upper, lower = (edges[i], there) if f < 2 else (there, edges[i])
            (hi0, lo0), (hi1, lo1) = upper, lower
            t.append(dot(fyb[...], jnp.concatenate([hi0, hi1, lo0, lo1, hi0, hi1], axis=0)))
        ts.append(t)
    correlate(ts, 1, lambda cam, r: 3 + 24 * cam, lambda cam, r: 3 + cam)

    hi, mid, lo = split3(stats[...])
    y = dot(jnp.concatenate([hi, mid, lo], axis=0), to_window)
    y = y[0:40] + y[40:80] + y[80:120]
    across = window[0:1] >= 48
    y_above = y[32:40]
    y = sum(jnp.where(window // 16 == r, y[8 * r : 8 * r + 8], 0.0) for r in range(4))

    def displacement(y, peak, cam):
        inverse = 1.0 / y[cam : cam + 1]
        return [
            peak[2 * cam + part : 2 * cam + part + 1]
            + y[2 + 2 * part + cam : 3 + 2 * part + cam] * inverse
            for part in range(2)
        ]

    def six_rows(calib, disp, live):
        vec = []
        for i in range(3):
            vec.append(sum(calib[4 * i + j : 4 * i + j + 1] * d for j, d in disp) * live)
            vec.append(vec[-1])
        return jnp.concatenate(vec + [jnp.zeros((2, 128), F32)], axis=0)

    disp = displacement(y, peak2, 0)
    disp += [jnp.where(across, 0.0, d) for d in displacement(y, peak2, 1)]
    own = six_rows(calib2, list(enumerate(disp)), live[0:1])
    disp = displacement(y_above, peak_above, 1)
    other = six_rows(calib_above, list(enumerate(disp, 2)), jnp.where(across, live_above, 0.0))
    left = iota((8, 128), 1) < WINS
    vecs[pl.ds(tm, 1)] = jnp.where(left, own, other)[None]

    def vec_copy(i):
        peer = lax.rem(tm + i, N_TM)
        return pltpu.make_async_remote_copy(
            src_ref=vecs.at[tm],
            dst_ref=vecs.at[tm],
            send_sem=vec_send,
            recv_sem=vec_recv,
            device_id=(peer, tile),
            device_id_type=MESH,
        )

    for i in range(1, N_TM):
        vec_copy(i).start()

    pltpu.make_async_copy(vecs.at[pl.ds(0, 7)], vecs.at[pl.ds(0, 7)], vec_send).wait()
    pl.semaphore_wait(round_sem, 2)
    pltpu.make_async_copy(vecs.at[pl.ds(0, 7)], vecs.at[pl.ds(0, 7)], vec_recv).wait()
    own, other = [], []
    for k in range(2):
        total = sum(coefs[k * N_TM + s] * vecs[s] for s in range(N_TM))
        turned = pltpu.roll(total, WINS, 1)
        own.append(jnp.where(left, total, turned))
        other.append(jnp.where(left, turned, total))

    first = iota((32, 128), 1) < WINS
    blank = jnp.zeros((WINS, 128), F32)

    def message(place, payload):
        both = jnp.concatenate(
            [jnp.where(first, payload, 0.0), jnp.where(first, 0.0, payload)], axis=0
        )
        table = jnp.concatenate(
            [jnp.concatenate([both, blank], axis=0), jnp.concatenate([blank, both], axis=0)], axis=1
        )
        return sum(dot_t(place, piece) for piece in split2(table))

    payload = jnp.concatenate(own + [spread2, cells], axis=0)
    payload_above = jnp.concatenate(other + [jnp.zeros((16, 128), F32)], axis=0)
    outbox[:, 0:1] = message(place, payload).reshape(N_TILE, 1, 128)
    outbox[:, 1:2] = message(place_above, payload_above).reshape(N_TILE, 1, 128)

    mine = pltpu.make_async_copy(outbox.at[tile], inbox.at[tile], load_sem)
    mine.start()

    def box_copy(i):
        peer = lax.rem(tile + i, N_TILE)
        return pltpu.make_async_remote_copy(
            src_ref=outbox.at[peer],
            dst_ref=inbox.at[tile],
            send_sem=box_send,
            recv_sem=box_recv,
            device_id=(tm, peer),
            device_id_type=MESH,
        )

    def send_box(i, carry):
        box_copy(i).start()
        return carry

    lax.fori_loop(1, N_TILE, send_box, 0)
    mine.wait()
    others = pl.ds(0, N_TILE - 1)
    pltpu.make_async_copy(outbox.at[others], outbox.at[others], box_send).wait()
    pltpu.make_async_copy(inbox.at[others], inbox.at[others], box_recv).wait()
    first, second = inbox[:, 0], inbox[:, 1]
    got_ref[...] = first + jnp.concatenate([second[1:], second[:1]], axis=0)


def deposit(got_ref, out_ref):
    got = got_ref[...]
    slots = jnp.concatenate(
        [got] + [pltpu.roll(got, 128 - 32 * c, 1) for c in range(1, CAP)], axis=0
    )
    cells = slots[:, 24:25].astype(jnp.int32)
    dist = (iota((128, AZ), 1) - cells) & (AZ - 1)
    weights = jnp.zeros((128, AZ), F32)
    for k in range(SPREAD):
        weights = jnp.where(dist == k, slots[:, 16 + k : 17 + k], weights)
    w_hi, w_lo = split2(weights)
    across = slots.T
    values = jnp.where(iota((16, 128), 0) == 6, 1.0, across[0:16])
    band = across[24:25].astype(jnp.int32) // AZ
    lhs_hi, lhs_lo = split2(
        jnp.concatenate([jnp.where(band == r, values, 0.0) for r in range(4)], axis=0)
    )
    num = dot(
        jnp.concatenate([lhs_hi, lhs_hi], axis=1), jnp.concatenate([w_hi, w_lo], axis=0)
    ) + dot(lhs_lo, w_hi)
    for r in range(4):
        block = num[16 * r : 16 * r + 16]
        scale = 1.0 / jnp.maximum(block[6:7], 1.0)
        for k in range(2):
            terms = (block[8 * k : 8 * k + 6] * scale).reshape(3, 2, AZ)
            out_ref[3 * k : 3 * k + 3, :, r * AZ : (r + 1) * AZ] = terms


def on_device(frames, peaks, calib, counts, owner, cell, spread, start):
    tables = [jnp.asarray(t) for t in _tables()]
    vmem, hbm = pl.BlockSpec(memory_space=pltpu.VMEM), pl.BlockSpec(memory_space=pltpu.HBM)
    smem = pl.BlockSpec(memory_space=pltpu.SMEM)
    width = frames.shape[3]
    inputs = (
        *tables, peaks, calib, owner.reshape(1, -1), cell.reshape(1, -1), spread
    )
    got = pl.pallas_call(
        correlate_and_send,
        out_shape=jax.ShapeDtypeStruct((N_TILE, 128), F32),
        in_specs=[smem, smem] + [hbm] * 12,
        out_specs=vmem,
        scratch_shapes=[
            pltpu.VMEM(x.shape, x.dtype) for x in inputs
        ]
        + [
            pltpu.VMEM((4, 128, width), BF),
            pltpu.VMEM((2, HALF, width), BF),
            pltpu.VMEM((2, HALF, width), BF),
            pltpu.VMEM((24, 128), F32),
            pltpu.VMEM((24, 128), F32),
            pltpu.VMEM((32, width), F32),
            pltpu.VMEM((40, width), F32),
            pltpu.VMEM((N_TM, 8, 128), F32),
            pltpu.VMEM((N_TILE, 2, 128), F32),
            pltpu.VMEM((N_TILE, 2, 128), F32),
        ]
        + [pltpu.SemaphoreType.DMA] * 5
        + [pltpu.SemaphoreType.DMA((3,))] * 2
        + [pltpu.SemaphoreType.DMA((11,)), pltpu.SemaphoreType.REGULAR],
        compiler_params=pltpu.CompilerParams(
            collective_id=0, has_side_effects=True, vmem_limit_bytes=63 * 1024 * 1024
        ),
    )(counts, start, frames, *inputs)
    spectrum = pl.pallas_call(
        deposit,
        out_shape=jax.ShapeDtypeStruct((6, 2, 4 * AZ), F32),
        in_specs=[vmem],
        out_specs=vmem,
        compiler_params=pltpu.CompilerParams(vmem_limit_bytes=63 * 1024 * 1024),
    )(got)
    return spectrum.transpose(1, 0, 2)


def solution(mesh):
    return jax.shard_map(
        on_device,
        mesh=mesh,
        in_specs=(
            P("tm", None, "tile", None),
            P("tm", None, "tile"),
            P(None, "tile"),
            P("tile"),
            P("tile", None),
            P("tile"),
            P(None, "tile"),
            P(),
        ),
        out_specs=P("tm", None, "tile"),
        check_vma=False,
    )
```

```python
import itertools
import math

import jax
import jax.numpy as jnp
import ml_dtypes
import numpy as np
from jax import lax
from jax.experimental import pallas as pl
from jax.experimental.pallas import tpu as pltpu
from jax.sharding import PartitionSpec as P

WIN = 64
HALF = 32
FREQS = 16
NFFT = 4096
AZ = 512
SPREAD = 8
CAP = 4
GROUP = 256
WINS = 64
SHARPNESS = 20.0
MESH = pl.DeviceIdType.MESH
BF = jnp.bfloat16
F32 = jnp.float32
N_TM = 8
N_TILE = 32


def _pair(table):
    hi = table.astype(ml_dtypes.bfloat16)
    lo = (table - hi.astype(np.float64)).astype(ml_dtypes.bfloat16)
    return hi, lo


def _real_dft():
    n = np.arange(WIN)
    k = np.arange(HALF)[:, None]
    cos = np.round(np.cos(2.0 * np.pi * ((k * n) % WIN) / WIN), 14)
    sin = np.round(np.sin(2.0 * np.pi * ((k * n) % WIN) / WIN), 14)
    sin[0] = 1.0 - 2.0 * (n % 2)
    return cos, sin


def _tables():
    cos, sin = _real_dft()
    weight = np.where(np.arange(HALF) == 0, 1.0, 2.0)[:, None]
    eye = np.eye(4)
    fx = np.concatenate([np.kron(eye, cos.T), np.kron(eye, sin.T)], axis=1)
    ix = np.concatenate([np.kron(eye, weight * cos), np.kron(eye, weight * sin)], axis=0)
    fy = np.zeros((2, 3, HALF, 128))
    for r in range(3):
        fy[0, r, :, r * HALF : r * HALF + WIN] = cos
        fy[1, r, :, r * HALF : r * HALF + WIN] = sin
    fy = fy.reshape(192, 128)
    fyb = np.concatenate([cos, sin], axis=0)
    iy = np.concatenate([weight * cos, weight * sin], axis=0).T
    fx_hi, fx_lo = _pair(fx)
    ix_hi, ix_lo = _pair(ix)
    fy_hi, fy_lo = _pair(fy)
    fyb_hi, fyb_lo = _pair(fyb)
    iy_hi, iy_lo = _pair(iy)
    cat = np.concatenate
    halves = slice(0, HALF), slice(HALF, WIN)
    return (
        np.stack([fx_hi, fx_lo]),
        np.stack([ix_hi, ix_lo]),
        cat([fy_hi, fy_hi], axis=1),
        fy_lo,
        np.stack([cat([fyb_hi[:, h], fyb_hi[:, h], fyb_lo[:, h]], axis=1) for h in halves]),
        cat([iy_hi, iy_hi, iy_lo], axis=1),
    )


def dot(lhs, rhs):
    return jnp.dot(lhs, rhs, preferred_element_type=F32)


def dot_t(lhs, rhs):
    return lax.dot_general(lhs, rhs, (((1,), (1,)), ((), ())), preferred_element_type=F32)


def split2(x):
    hi = x.astype(BF)
    return hi, (x - hi.astype(F32)).astype(BF)


def split3(x):
    hi = x.astype(BF)
    rest = x - hi.astype(F32)
    mid = rest.astype(BF)
    return hi, mid, (rest - mid.astype(F32)).astype(BF)


def iota(shape, dim):
    return lax.broadcasted_iota(jnp.int32, shape, dim)


def cross(first, second, y0, x0):
    a, b, c, d = first
    a2, b2, c2, d2 = second
    aa, bb, cc, dd = a * a2, b * b2, c * c2, d * d2
    ac, bd = a * c2 - c * a2, b * d2 - d * b2
    ab, cd = a * b2 - b * a2, c * d2 - d * c2
    ad, bc = a * d2 + d * a2, b * c2 + c * b2
    low, high = jnp.where(x0, aa, aa + cc), jnp.where(x0, bb, bb + dd)
    low_s, high_s = jnp.where(x0, cc, ac), jnp.where(x0, dd, bd)
    p_cc = jnp.where(y0, low, low + high)
    p_cs = jnp.where(y0, low_s, jnp.where(x0, cc + dd, ac + bd))
    p_sc = jnp.where(y0, high, jnp.where(x0, ab, ab + cd))
    p_ss = jnp.where(y0, high_s, jnp.where(x0, cd, ad - bc))
    return p_cc, p_cs, p_sc, p_ss


def parts(t, half):
    return t[:half, :128], t[half:, :128], t[:half, 128:], t[half:, 128:]


def inverse_x(spectra, ix):
    rows = []
    for p_cc, p_cs, p_sc, p_ss in spectra:
        rows.append(jnp.concatenate([p_cc, p_cs], axis=1))
        rows.append(jnp.concatenate([p_sc, p_ss], axis=1))
    hi, lo = split2(jnp.concatenate(rows, axis=0))
    return dot(hi, ix[0]) + dot(lo, ix[0]) + dot(hi, ix[1])


def energy_rows(four, weight, bands):
    a, b, c, d = four
    e = (a * a + b * b) + (c * c + d * d)
    return [
        jnp.sum(e[r * HALF : (r + 1) * HALF] * weight, axis=0, keepdims=True) for r in range(bands)
    ]


def inverse_norm(rows, spread_lanes):
    have = len(rows)
    padded = rows + [jnp.zeros((16 - have, 128), F32)] * (have < 16)
    hi, mid, lo = split3(jnp.concatenate(padded, axis=0))
    wide = dot(jnp.concatenate([hi, mid, lo], axis=0), spread_lanes)
    total = wide[0:16] + wide[16:32] + wide[32:48]
    return lax.rsqrt(total * (1.0 / 4096.0**2) + 1e-5)


def wrapped(lag, peak):
    off = lag - peak
    return jnp.where(off >= 32.0, off - 64.0, off)


def correlate_and_send(
    counts, start, frames, *refs,
):
    hbm_inputs, got_ref, inputs = refs[:11], refs[11], refs[12:23]
    fx, ix, fy2, fy_lo, fyb, iy, peaks, calib, owner, cell, spread = inputs
    image, from_below, from_above, pack, pack_in, peak_lanes, stats, vecs, outbox, inbox = refs[23:33]
    load_sem, vec_send, vec_recv, box_send, box_recv, halo_send, halo_recv, input_sems, round_sem = (
        refs[33:]
    )
    tm, tile = lax.axis_index("tm"), lax.axis_index("tile")
    above, below = lax.rem(tile + N_TILE - 1, N_TILE), lax.rem(tile + 1, N_TILE)

    loads = [
        pltpu.make_async_copy(source, target, input_sems.at[i])
        for i, (source, target) in enumerate(zip(hbm_inputs, inputs))
    ]
    load = pltpu.make_async_copy(frames.at[0], image, load_sem)
    for one in loads[6:]:
        one.start()
    load.start()
    for one in loads[:6]:
        one.start()

    barrier = pltpu.get_barrier_semaphore()

    def greet(sem, d_tm, d_tile):
        peer = (lax.rem(tm + d_tm, N_TM), lax.rem(tile + d_tile, N_TILE))
        pl.semaphore_signal(sem, 1, device_id=peer, device_id_type=MESH)

    near = [d % N_TILE for i in range(1, 9) for d in (i, -i)]
    for d in near:
        greet(barrier, 0, d)
    for d in range(1, N_TM):
        greet(barrier, d, 0)

    pl.semaphore_wait(barrier, len(near) + N_TM - 1)
    for d in (8, N_TILE - 8):
        greet(round_sem, 0, d)
    def to_tile(peer, source, target, i):
        return pltpu.make_async_remote_copy(
            src_ref=source,
            dst_ref=target,
            send_sem=halo_send.at[i],
            recv_sem=halo_recv.at[i],
            device_id=(tm, peer),
            device_id_type=MESH,
        )

    halos = [
        to_tile(above, frames.at[0, pl.ds(0, 2), pl.ds(0, HALF), :], from_below, 0),
        to_tile(below, frames.at[0, pl.ds(2, 2), pl.ds(96, HALF), :], from_above, 1),
        to_tile(below, pack, pack_in, 2),
    ]
    halos[0].start()
    halos[1].start()
    for one in loads[6:]:
        one.wait()

    def twice(x):
        return jnp.concatenate([x, x], axis=1)

    window = iota((8, 128), 1) % WINS
    live = (window >= WINS - counts[0]).astype(F32)
    peak2, calib2 = twice(peaks[0].astype(F32)), twice(calib[...])
    owner2 = twice(owner[...].astype(F32))
    pack[0:16] = jnp.concatenate([calib2, peak2], axis=0)
    pack[16:24] = jnp.concatenate([owner2, live[0:7]], axis=0)
    halos[2].start()

    stats[...] = jnp.zeros_like(stats)
    band_of = iota((4, WINS), 1) // 16
    to_lanes = (iota((WINS, 1024), 0) % 16 == iota((WINS, 1024), 1) // WIN).astype(F32).astype(BF)

    def lanes_of_peaks(peak):
        picks = [
            jnp.where(
                iota((4, WINS), 0) == band_of, jnp.broadcast_to(peak[j : j + 1, :WINS], (4, WINS)), 0.0
            )
            for j in range(4)
        ]
        return dot(jnp.concatenate(picks, axis=0).astype(BF), to_lanes)

    peak_lanes[0:16] = lanes_of_peaks(peak2)

    for one in loads[:6]:
        one.wait()
    load.wait()

    weight = jnp.where(iota((HALF, 128), 0) == 0, 1.0, 2.0) * jnp.where(
        iota((HALF, 128), 1) % HALF == 0, 1.0, 2.0
    )
    spread_lanes = (iota((128, GROUP), 0) // HALF == iota((128, GROUP), 1) // WIN).astype(F32)
    spread_lanes = spread_lanes.astype(BF)
    row_lag = iota((WIN, GROUP), 0).astype(F32)
    col_lag = (iota((1, GROUP), 1) % WIN).astype(F32)
    gain = SHARPNESS * math.log2(math.e) / 4096.0**2

    def slots(bands):
        shape = (bands * HALF, 128)
        y0, x0 = iota(shape, 0) % HALF == 0, iota(shape, 1) % HALF == 0
        return y0, x0, y0 & x0

    def correlate(ts, bands, at_lanes, at_stats):
        half = bands * HALF
        y0, x0, dc = slots(bands)
        scales, spectra = [], []
        for t in ts:
            four = []
            for one in t:
                a, b, c, d = parts(one, half)
                four.append((jnp.where(dc, 0.0, a), b, c, d))
            energies = [row for one in four for row in energy_rows(one, weight, bands)]
            scales.append(inverse_norm(energies, spread_lanes))
            spectra += [cross(four[2 * cam], four[2 * cam + 1], y0, x0) for cam in range(2)]
        z_hi, z_lo = split2(inverse_x(spectra, ix))
        for g, cam, r in itertools.product(range(len(ts)), range(2), range(bands)):
            lanes, scale = slice(g * GROUP, (g + 1) * GROUP), scales[g]
            at = [((g * 2 + cam) * 2 + part) * half + r * HALF for part in range(2)]
            hi = [z_hi[i : i + HALF] for i in at]
            lo = [z_lo[i : i + HALF] for i in at]
            corr = dot(iy[...], jnp.concatenate(hi + lo + hi, axis=0))
            i, j = (2 * cam) * bands + r, (2 * cam + 1) * bands + r
            p = jnp.exp2(corr * (scale[i : i + 1] * scale[j : j + 1] * gain))
            i = at_lanes(cam, r)
            rows_at, cols_at = peak_lanes[i : i + 1, lanes], peak_lanes[i + 4 : i + 5, lanes]
            total = jnp.sum(p, axis=0, keepdims=True)
            by_row = jnp.sum(p * wrapped(row_lag, rows_at), axis=0, keepdims=True)
            by_col = total * wrapped(col_lag, cols_at)
            for k, value in enumerate((total, by_row, by_col)):
                i = at_stats(cam, r) * 8 + k * 2 + cam
                stats[i : i + 1, lanes] = value

    def x_transform(blocks):
        rows = [block[:, g * GROUP : (g + 1) * GROUP] for g in range(4) for block in blocks]
        pixels = jnp.concatenate(rows, axis=0)
        return dot(pixels, fx[0]) + dot(pixels, fx[1])

    last, first = tile == N_TILE - 1, tile == 0
    mean_lane = (iota((1, GROUP), 1) < 128) & (iota((1, GROUP), 1) % HALF == 0)
    x = x_transform([image[f] for f in range(4)])
    ts, edges, levels = [], [], []
    for g in range(4):
        t = []
        for f in range(4):
            at = (g * 4 + f) * 128
            level = jnp.where(mean_lane, x[at : at + 1], 0.0)
            hi, lo = split2(x[at : at + 128] - level)
            levels.append(level)
            top = jnp.where(first, 0.0, x[at : at + HALF]) - level
            edges.append((hi[96:], lo[96:]) if f < 2 else split2(top))
            t.append(dot(fy2[...], jnp.concatenate([hi, lo], axis=0)) + dot(fy_lo[...], hi))
        ts.append(t)
    correlate(ts, 3, lambda cam, r: 8 * cam + r, lambda cam, r: r)

    to_window = (iota((1024, 128), 0) // WIN == iota((1024, 128), 1) % 16).astype(F32).astype(BF)
    before = (iota((128, 128), 0) < iota((128, 128), 1) % WINS) & (iota((128, 128), 0) < WINS)
    before = before.astype(F32).astype(BF)
    half = (iota((1, 128), 1) // WINS).astype(F32)

    def places(owners):
        hits = (owners.astype(jnp.int32) == iota((N_TILE, 128), 0)).astype(F32)
        rank = jnp.sum(hits * dot(hits.astype(BF), before), axis=0, keepdims=True)
        both = [jnp.where(rank == half, hits, 0.0), jnp.where(rank == half + 2.0, hits, 0.0)]
        return jnp.concatenate(both, axis=1).astype(BF)

    place = places(owner2)
    cells = jnp.broadcast_to(twice(cell[...].astype(F32)), (8, 128))
    spread2 = twice(spread[...]) * live
    freq = tm * 2 + (iota((8, 128), 0) & 1)
    coefs = []
    for k in range(2):
        for s in range(N_TM):
            n = (freq * (start[0] + s) + 4 * k) & 15
            value = jnp.zeros((8, 128), F32)
            for step in range(16):
                value = jnp.where(n == step, math.cos(2.0 * math.pi * step / 16), value)
            coefs.append(value)

    def half_transform(half, hi, lo):
        return dot(fyb[half], jnp.concatenate([hi, lo, hi], axis=0))

    here = [half_transform(int(i % 4 >= 2), *edge) for i, edge in enumerate(edges)]

    halos[2].wait()
    place_above = places(pack_in[16:17])
    peak_above, calib_above, live_above = pack_in[12:16], pack_in[0:12], pack_in[17:18]
    peak_lanes[16:32] = lanes_of_peaks(peak_above)

    halos[0].wait()
    halos[1].wait()
    x = x_transform([from_below[0], from_below[1], from_above[0], from_above[1]])
    keep = jnp.where(last, 0.0, 1.0)
    ts = []
    for g in range(4):
        t = []
        for f in range(4):
            i = g * 4 + f
            part = x[i * HALF : (i + 1) * HALF]
            there = split2((part * keep if f < 2 else part) - levels[i])
            t.append(here[i] + half_transform(int(f < 2), *there))
        ts.append(t)
    correlate(ts, 1, lambda cam, r: 3 + 24 * cam, lambda cam, r: 3 + cam)

    hi, mid, lo = split3(stats[...])
    y = dot(jnp.concatenate([hi, mid, lo], axis=0), to_window)
    y = y[0:40] + y[40:80] + y[80:120]
    across = window[0:1] >= 48
    y_above = y[32:40]
    y = sum(jnp.where(window // 16 == r, y[8 * r : 8 * r + 8], 0.0) for r in range(4))

    def displacement(y, peak, cam):
        inverse = 1.0 / y[cam : cam + 1]
        return [
            peak[2 * cam + part : 2 * cam + part + 1]
            + y[2 + 2 * part + cam : 3 + 2 * part + cam] * inverse
            for part in range(2)
        ]

    def six_rows(calib, disp, live):
        vec = []
        for i in range(3):
            vec.append(sum(calib[4 * i + j : 4 * i + j + 1] * d for j, d in disp) * live)
            vec.append(vec[-1])
        return jnp.concatenate(vec + [jnp.zeros((2, 128), F32)], axis=0)

    disp = displacement(y, peak2, 0)
    disp += [jnp.where(across, 0.0, d) for d in displacement(y, peak2, 1)]
    own = six_rows(calib2, list(enumerate(disp)), live[0:1])
    disp = displacement(y_above, peak_above, 1)
    other = six_rows(calib_above, list(enumerate(disp, 2)), jnp.where(across, live_above, 0.0))
    left = iota((8, 128), 1) < WINS
    vecs[pl.ds(tm, 1)] = jnp.where(left, own, other)[None]

    def vec_copy(i):
        peer = lax.rem(tm + i, N_TM)
        return pltpu.make_async_remote_copy(
            src_ref=vecs.at[tm],
            dst_ref=vecs.at[tm],
            send_sem=vec_send,
            recv_sem=vec_recv,
            device_id=(peer, tile),
            device_id_type=MESH,
        )

    for i in range(1, N_TM):
        vec_copy(i).start()

    pltpu.make_async_copy(vecs.at[pl.ds(0, 7)], vecs.at[pl.ds(0, 7)], vec_send).wait()
    pl.semaphore_wait(round_sem, 2)
    pltpu.make_async_copy(vecs.at[pl.ds(0, 7)], vecs.at[pl.ds(0, 7)], vec_recv).wait()
    own, other = [], []
    for k in range(2):
        total = sum(coefs[k * N_TM + s] * vecs[s] for s in range(N_TM))
        turned = pltpu.roll(total, WINS, 1)
        own.append(jnp.where(left, total, turned))
        other.append(jnp.where(left, turned, total))

    first = iota((32, 128), 1) < WINS
    blank = jnp.zeros((WINS, 128), F32)

    def message(place, payload):
        both = jnp.concatenate(
            [jnp.where(first, payload, 0.0), jnp.where(first, 0.0, payload)], axis=0
        )
        table = jnp.concatenate(
            [jnp.concatenate([both, blank], axis=0), jnp.concatenate([blank, both], axis=0)], axis=1
        )
        return sum(dot_t(place, piece) for piece in split2(table))

    payload = jnp.concatenate(own + [spread2, cells], axis=0)
    payload_above = jnp.concatenate(other + [jnp.zeros((16, 128), F32)], axis=0)
    outbox[:, 0:1] = message(place, payload).reshape(N_TILE, 1, 128)
    outbox[:, 1:2] = message(place_above, payload_above).reshape(N_TILE, 1, 128)

    mine = pltpu.make_async_copy(outbox.at[tile], inbox.at[tile], load_sem)
    mine.start()

    def box_copy(i):
        peer = lax.rem(tile + i, N_TILE)
        return pltpu.make_async_remote_copy(
            src_ref=outbox.at[peer],
            dst_ref=inbox.at[tile],
            send_sem=box_send,
            recv_sem=box_recv,
            device_id=(tm, peer),
            device_id_type=MESH,
        )

    def send_box(i, carry):
        box_copy(i).start()
        return carry

    lax.fori_loop(1, N_TILE, send_box, 0)
    mine.wait()
    others = pl.ds(0, N_TILE - 1)
    pltpu.make_async_copy(outbox.at[others], outbox.at[others], box_send).wait()
    pltpu.make_async_copy(inbox.at[others], inbox.at[others], box_recv).wait()
    first, second = inbox[:, 0], inbox[:, 1]
    got_ref[...] = first + jnp.concatenate([second[1:], second[:1]], axis=0)


def deposit(got_ref, out_ref):
    got = got_ref[...]
    slots = jnp.concatenate(
        [got] + [pltpu.roll(got, 128 - 32 * c, 1) for c in range(1, CAP)], axis=0
    )
    cells = slots[:, 24:25].astype(jnp.int32)
    dist = (iota((128, AZ), 1) - cells) & (AZ - 1)
    weights = jnp.zeros((128, AZ), F32)
    for k in range(SPREAD):
        weights = jnp.where(dist == k, slots[:, 16 + k : 17 + k], weights)
    w_hi, w_lo = split2(weights)
    across = slots.T
    values = jnp.where(iota((16, 128), 0) == 6, 1.0, across[0:16])
    band = across[24:25].astype(jnp.int32) // AZ
    lhs_hi, lhs_lo = split2(
        jnp.concatenate([jnp.where(band == r, values, 0.0) for r in range(4)], axis=0)
    )
    num = dot(
        jnp.concatenate([lhs_hi, lhs_hi], axis=1), jnp.concatenate([w_hi, w_lo], axis=0)
    ) + dot(lhs_lo, w_hi)
    for r in range(4):
        block = num[16 * r : 16 * r + 16]
        scale = 1.0 / jnp.maximum(block[6:7], 1.0)
        for k in range(2):
            terms = (block[8 * k : 8 * k + 6] * scale).reshape(3, 2, AZ)
            out_ref[3 * k : 3 * k + 3, :, r * AZ : (r + 1) * AZ] = terms


def on_device(frames, peaks, calib, counts, owner, cell, spread, start):
    tables = [jnp.asarray(t) for t in _tables()]
    vmem, hbm = pl.BlockSpec(memory_space=pltpu.VMEM), pl.BlockSpec(memory_space=pltpu.HBM)
    smem = pl.BlockSpec(memory_space=pltpu.SMEM)
    width = frames.shape[3]
    inputs = (
        *tables, peaks, calib, owner.reshape(1, -1), cell.reshape(1, -1), spread
    )
    got = pl.pallas_call(
        correlate_and_send,
        out_shape=jax.ShapeDtypeStruct((N_TILE, 128), F32),
        in_specs=[smem, smem] + [hbm] * 12,
        out_specs=vmem,
        scratch_shapes=[
            pltpu.VMEM(x.shape, x.dtype) for x in inputs
        ]
        + [
            pltpu.VMEM((4, 128, width), BF),
            pltpu.VMEM((2, HALF, width), BF),
            pltpu.VMEM((2, HALF, width), BF),
            pltpu.VMEM((24, 128), F32),
            pltpu.VMEM((24, 128), F32),
            pltpu.VMEM((32, width), F32),
            pltpu.VMEM((40, width), F32),
            pltpu.VMEM((N_TM, 8, 128), F32),
            pltpu.VMEM((N_TILE, 2, 128), F32),
            pltpu.VMEM((N_TILE, 2, 128), F32),
        ]
        + [pltpu.SemaphoreType.DMA] * 5
        + [pltpu.SemaphoreType.DMA((3,))] * 2
        + [pltpu.SemaphoreType.DMA((11,)), pltpu.SemaphoreType.REGULAR],
        compiler_params=pltpu.CompilerParams(
            collective_id=0, has_side_effects=True, vmem_limit_bytes=63 * 1024 * 1024
        ),
    )(counts, start, frames, *inputs)
    spectrum = pl.pallas_call(
        deposit,
        out_shape=jax.ShapeDtypeStruct((6, 2, 4 * AZ), F32),
        in_specs=[vmem],
        out_specs=vmem,
        compiler_params=pltpu.CompilerParams(vmem_limit_bytes=63 * 1024 * 1024),
    )(got)
    return spectrum.transpose(1, 0, 2)


def solution(mesh):
    return jax.shard_map(
        on_device,
        mesh=mesh,
        in_specs=(
            P("tm", None, "tile", None),
            P("tm", None, "tile"),
            P(None, "tile"),
            P("tile"),
            P("tile", None),
            P("tile"),
            P(None, "tile"),
            P(),
        ),
        out_specs=P("tm", None, "tile"),
        check_vma=False,
    )
```
